128 devices in a mesh: dom: 32 (over y, z, core), feat: 4 (over x).
Axes of the slice: x: 4, y: 4, z: 4, core: 2. Of those that a mesh axis runs over, the one named last changes fastest.
Arguments:
- features: bfloat16 [262144, 128], P('dom'), may hold values from -6 to 6
- weight: bfloat16 [128, 256], P(None, 'feat'), may hold values from -0.5 to 0.5
- attention: float32 [2, 4, 64], P(None, 'feat')
- bias: float32 [256], P('feat'), may hold values from -3 to 3
- cotangent: bfloat16 [256, 262144], P('feat', 'dom'), may hold values from -0.01171875 to 0.01171875
- local_pairs: int32 [2048, 5], P('dom'), may hold values from 0 to 63, as said below
- local_counts: int32 [2048, 5, 128], P('dom'), may hold values from 0 to 6
- remote_pairs: int32 [2048, 3], P('dom'), may hold values from 0 to 63, as said below
- remote_counts: int32 [2048, 3, 128], P('dom'), may hold values from 0 to 6
- send_rows: int32 [32, 32, 256], P('dom'), may hold values from 0 to 8191
- send_counts: int32 [32, 32], replicated, may hold values from 1 to 256
Outputs:
- output: bfloat16 [256, 262144], P('feat', 'dom')
- grad_weight: float32 [128, 256], P(None, 'feat')
- grad_attention: float32 [2, 4, 64], P(None, 'feat')
- grad_bias: float32 [256], P('feat')
The draws below stay inside these ranges and needn't reach their ends.
Inputs may be any that keep to these rules, and one draw needn't show every extreme that they name: `local_pairs`: the 5 blocks of a row are different. `remote_pairs`: the 3 entries of a row are different.
All inputs are finite; a program needn't handle non-finite values.
Results may differ from the reference program's by a relative error of at most 0.0035.
The reference program's roundings to bfloat16 on the way count: a program that leaves them out, or rounds other values in their place, can miss the bound.
Values may be sent and summed in bfloat16 or wider, within the bound.
No kernel may reach another device: no remote copies, remote signals or barrier semaphores. Data moves between devices by JAX's collectives and lax.ppermute only.
A program may use at most 64 MiB of HBM per device.

```python
import jax
import jax.numpy as jnp
from jax import lax

F_IN = 128
HEADS = 4
HEAD = 64
BLK = 128
PEER_BLOCKS = 2
LOCAL_PAIRS = 5
REMOTE_PAIRS = 3
NODE_DEV = 8192
WIDTH = 256
NODES = 262144
BLOCKS = 2048
CAP = 256
N_DOM = 32


def draw_attention(key, part):
    key = jax.random.fold_in(key, 1)
    spread = 0.15
    return jax.random.normal(key, (2, HEADS, HEAD), jnp.float32) * spread


def distinct_choice(key, rows, among, taken):
    raw_scores = jax.random.randint(key, (rows, among), 0, 2 ** 20, dtype=jnp.int32)
    keyed = raw_scores * among + jnp.arange(among, dtype=jnp.int32)[None, :]
    return jnp.argsort(keyed, axis=1)[:, :taken].astype(jnp.int32)


def draw_local_pairs(key, part):
    key = jax.random.fold_in(key, 2)
    return distinct_choice(key, BLOCKS, NODE_DEV // BLK, LOCAL_PAIRS)


def draw_remote_pairs(key, part):
    key = jax.random.fold_in(key, 3)
    return distinct_choice(key, BLOCKS, N_DOM * PEER_BLOCKS, REMOTE_PAIRS)


def draw_local_counts(key, part):
    key = jax.random.fold_in(key, 4)
    counted = jax.random.randint(key, (BLOCKS, LOCAL_PAIRS, BLK), 0, 7, dtype=jnp.int32)
    return counted.at[0, 0, 0].set(6).at[0, 0, 1].set(0)


def draw_remote_counts(key, part):
    key = jax.random.fold_in(key, 5)
    counted = jax.random.randint(key, (BLOCKS, REMOTE_PAIRS, BLK), 0, 7, dtype=jnp.int32)
    return counted.at[0, 0, 0].set(6).at[0, 0, 1].set(0)


def draw_send_counts(key, part):
    key = jax.random.fold_in(key, 6)
    counted = jax.random.randint(key, (N_DOM, N_DOM), 1, CAP + 1, dtype=jnp.int32)
    return counted.at[0, 0].set(CAP)


def touch_ends(values, rng, smallest, high):
    longest = values.shape.index(max(values.shape))
    spots = []
    for shift in (0, 1):
        where = [jax.random.randint(jax.random.fold_in(rng, axis), (), 0, length) for axis, length in enumerate(values.shape)]
        where[longest] = (where[longest] + shift) % values.shape[longest]
        spots.append(tuple(where))
    return values.at[spots[0]].set(smallest).at[spots[1]].set(high)


def level_of(own_key, extent, shards, low, top_value):
    gain, own = 1.0, jax.random.fold_in(own_key, 6)
    for dim, parts in shards:
        draws = jnp.exp(jax.random.uniform(jax.random.fold_in(own, dim), (parts,), jnp.float32, low / len(shards), top_value / len(shards)))
        gain = gain * jnp.repeat(draws, extent[dim] // parts).reshape([-1 if axis == dim else 1 for axis in range(len(extent))])
    return gain


def centred(key, shape, scale, reach, shards=(), kind=jnp.bfloat16):
    gain = level_of(key, shape, shards, -0.22, 0.18) if shards else 1.0
    entries = jax.random.normal(key, shape, jnp.float32) * scale * gain
    return jnp.minimum(jnp.maximum(entries, -reach), reach).astype(kind)


def setup_inputs(seed: int = 0) -> dict:
    arg_keys = jax.random.split(jax.random.key(seed), 12)
    return {
        "features": centred(arg_keys[0], (NODES, F_IN), 1.0, 6.0, ((0, 32),)),
        "weight": centred(arg_keys[1], (F_IN, WIDTH), F_IN ** -0.5, 0.5, ((1, 4),)),
        "attention": draw_attention(jax.random.fold_in(arg_keys[11], 71), 0),
        "bias": centred(arg_keys[3], (WIDTH,), 0.5, 3.0, ((0, 4),), jnp.float32),
        "cotangent": centred(arg_keys[4], (WIDTH, NODES), (NODES ** -0.5), 0.01171875, ((0, 4), (1, 32))),
        "local_pairs": draw_local_pairs(jax.random.fold_in(arg_keys[11], 71), 0),
        "local_counts": draw_local_counts(jax.random.fold_in(arg_keys[11], 71), 0),
        "remote_pairs": draw_remote_pairs(jax.random.fold_in(arg_keys[11], 71), 0),
        "remote_counts": draw_remote_counts(jax.random.fold_in(arg_keys[11], 71), 0),
        "send_rows": touch_ends(jax.random.randint(arg_keys[9], (N_DOM, N_DOM, CAP), 0, NODE_DEV), jax.random.fold_in(arg_keys[9], 1), 0, NODE_DEV - 1).astype(jnp.int32),
        "send_counts": draw_send_counts(jax.random.fold_in(arg_keys[11], 71), 0),
    }


def leaky_relu(values):
    return jnp.where(values > 0, values, 0.2 * values)


def slope_of(values):
    return jnp.where(values > 0, 1.0, 0.2)


def reference(features, weight, attention, bias, cotangent, local_pairs, local_counts, remote_pairs, remote_counts, send_rows, send_counts):
    node_count = features.shape[0]
    block_count = NODE_DEV // BLK
    projected = jnp.dot(features, weight, preferred_element_type=jnp.float32).astype(jnp.bfloat16).reshape(node_count, HEADS, HEAD)
    proj_float = projected.astype(jnp.float32)
    score_src = jnp.sum(proj_float * attention[0], axis=-1)
    score_dst = jnp.sum(proj_float * attention[1], axis=-1)
    upstream = cotangent.T.reshape(node_count, HEADS, HEAD).astype(jnp.float32)
    offsets = jnp.arange(BLK, dtype=jnp.int32)
    band = (offsets[None, None, :] - offsets[None, :, None]) % BLK
    bias_heads = bias.reshape(HEADS, HEAD)

    def one_block(carry, block):
        grad_rows, grad_scores = carry
        partition = block // block_count
        local_nodes = (partition * block_count + local_pairs[block])[:, None] * BLK + offsets[None, :]
        halo_blocks = remote_pairs[block]
        peer_ids = halo_blocks // PEER_BLOCKS
        peer_slots = ((halo_blocks % PEER_BLOCKS)[:, None] * BLK + offsets[None, :]).astype(jnp.int32)
        sent_rows = jnp.take_along_axis(send_rows[peer_ids, partition], peer_slots, axis=1)
        remote_nodes = peer_ids[:, None] * NODE_DEV + sent_rows
        remote_live = peer_slots < send_counts[peer_ids, partition][:, None]
        sources = jnp.concatenate([local_nodes, remote_nodes], 0).reshape(-1).astype(jnp.int32)
        source_live = jnp.concatenate([jnp.ones(local_nodes.shape, bool), remote_live], 0)
        edge_counts = jnp.concatenate([local_counts[block], remote_counts[block]], 0)
        valid = (band < edge_counts[:, :, None]) & source_live[:, None, :]
        valid = valid.transpose(1, 0, 2).reshape(BLK, -1)[None]
        targets = (block * BLK + offsets).astype(jnp.int32)
        source_proj = proj_float[sources]
        self_proj = proj_float[targets].transpose(1, 0, 2)
        dst_scores = score_dst[targets].T
        pre_logit = dst_scores[:, :, None] + score_src[sources].T[:, None, :]
        logits = leaky_relu(pre_logit)
        pre_self = dst_scores + score_src[targets].T
        logit_self = leaky_relu(pre_self)
        highest = jnp.maximum(jnp.max(jnp.where(valid, logits, -jnp.inf), axis=-1), logit_self)
        raised = jnp.where(valid, jnp.exp(logits - highest[..., None]), 0.0)
        raised_self = jnp.exp(logit_self - highest)
        denom = jnp.sum(raised, axis=-1) + raised_self
        weights_low = raised.astype(jnp.bfloat16).astype(jnp.float32)
        summed = jnp.einsum('hrs,shd->hrd', weights_low, source_proj)
        aggregate = (summed + raised_self[..., None] * self_proj) / denom[..., None]
        out_block = (aggregate + bias_heads[:, None, :]).astype(jnp.bfloat16)
        out_block = out_block.transpose(0, 2, 1).reshape(HEADS * HEAD, BLK)
        grad_out = upstream[targets].transpose(1, 0, 2)
        share = raised / denom[..., None]
        share_self = raised_self / denom
        grad_share = jnp.einsum('hrd,shd->hrs', grad_out, source_proj)
        inner = jnp.sum(grad_out * aggregate, axis=-1)
        grad_share_self = jnp.sum(grad_out * self_proj, axis=-1)
        grad_pre = share * (grad_share - inner[..., None]) * slope_of(pre_logit)
        grad_pre_self = share_self * (grad_share_self - inner) * slope_of(pre_self)
        grad_dst_block = jnp.sum(grad_pre, axis=-1) + grad_pre_self
        grad_src_block = jnp.sum(grad_pre, axis=1)
        share_low = share.astype(jnp.bfloat16).astype(jnp.float32)
        grad_sources = jnp.einsum('hrs,hrd->shd', share_low, grad_out)
        grad_rows = grad_rows.at[sources].add(grad_sources)
        grad_rows = grad_rows.at[targets].add((share_self[..., None] * grad_out).transpose(1, 0, 2))
        grad_scores = grad_scores.at[sources].add(grad_src_block.T)
        grad_scores = grad_scores.at[targets].add(grad_pre_self.T)
        return (grad_rows, grad_scores), (out_block, grad_dst_block.T)

    start = (jnp.zeros((node_count, HEADS, HEAD), jnp.float32), jnp.zeros((node_count, HEADS), jnp.float32))
    (grad_rows, grad_src), (out_blocks, grad_dst) = lax.scan(one_block, start, jnp.arange(BLOCKS, dtype=jnp.int32))
    output = out_blocks.transpose(1, 0, 2).reshape(HEADS * HEAD, node_count)
    grad_dst = grad_dst.reshape(node_count, HEADS)
    grad_projected = grad_rows + grad_src[..., None] * attention[0] + grad_dst[..., None] * attention[1]
    grad_weight = jnp.dot(features.astype(jnp.float32).T, grad_projected.reshape(node_count, HEADS * HEAD), precision=lax.Precision.HIGHEST)
    grad_attention = jnp.stack([jnp.sum(grad_src[..., None] * proj_float, axis=0), jnp.sum(grad_dst[..., None] * proj_float, axis=0)])
    grad_bias = jnp.sum(cotangent.astype(jnp.float32), axis=1)
    return output, grad_weight, grad_attention, grad_bias
```

```python
import jax
import jax.numpy as jnp
from jax import lax
from jax.experimental import pallas as pl
from jax.experimental.pallas import tpu as pltpu
from jax.sharding import PartitionSpec as P

BLK = 128
PEER_BLOCKS = 2
SUB = 8
LOW = jnp.bfloat16
WIDE = jnp.float32
VMEM_LIMIT = 56 * 1024 * 1024
SCRATCH_TURNS = 2
GATHER_STEP = 32


def gather_kernel(rows_ref, live_ref, features_ref, out_ref, wide_ref, stage_ref):
    node_count = features_ref.shape[0]
    peer_count, capacity = rows_ref.shape
    step_count = capacity // GATHER_STEP

    def widen(turn, carry):
        lead = pl.multiple_of(turn * BLK, BLK)
        wide_ref[pl.ds(lead, BLK), :] = features_ref[pl.ds(lead, BLK), :].astype(WIDE)
        return carry

    lax.fori_loop(0, node_count // BLK, widen, 0)

    def one_peer(peer, carry):
        busy = (live_ref[peer] + GATHER_STEP - 1) // GATHER_STEP

        def fetch(step, inner):
            lead = pl.multiple_of(peer * capacity + step * GATHER_STEP, GATHER_STEP)
            for slot in range(GATHER_STEP):
                row = rows_ref[peer, step * GATHER_STEP + slot]
                stage_ref[pl.ds(lead + slot, 1), :] = wide_ref[pl.ds(row, 1), :]
            return inner

        def blank(step, inner):
            lead = pl.multiple_of(peer * capacity + step * GATHER_STEP, GATHER_STEP)
            stage_ref[pl.ds(lead, GATHER_STEP), :] = jnp.zeros((GATHER_STEP, stage_ref.shape[1]), WIDE)
            return inner

        lax.fori_loop(0, busy, fetch, 0)
        lax.fori_loop(busy, step_count, blank, 0)
        return carry

    lax.fori_loop(0, peer_count, one_peer, 0)

    def narrow(turn, carry):
        lead = pl.multiple_of(turn * BLK, BLK)
        out_ref[pl.ds(lead, BLK), :] = stage_ref[pl.ds(lead, BLK), :].astype(LOW)
        return carry

    lax.fori_loop(0, peer_count * capacity // BLK, narrow, 0)


def spread(row):
    return jnp.broadcast_to(row, (SUB, BLK))


def layer_kernel(
    incoming_ref,
    local_pairs_ref,
    remote_pairs_ref,
    own_ref,
    halo_ref,
    weight_ref,
    consts_ref,
    cotangent_ref,
    local_counts_ref,
    remote_counts_ref,
    out_ref,
    shares_ref,
    proj_ref,
    projt_ref,
    score_ref,
    self_score_ref,
    dst_score_ref,
    grad_ref,
    grad_src_ref,
    grad_self_ref,
    grad_dst_ref,
    mask_ref,
    weights_ref,
    share_ref,
):
    block_count = own_ref.shape[0] // BLK
    halo_count = halo_ref.shape[0] // BLK
    local_count = local_pairs_ref.shape[1]
    remote_count = remote_pairs_ref.shape[1]
    pair_count = local_count + remote_count
    head_width = weight_ref.shape[1]

    sub_index = lax.broadcasted_iota(jnp.int32, (SUB, BLK), 0)
    lane_index = lax.broadcasted_iota(jnp.int32, (SUB, BLK), 1)
    step_index = (sub_index - lane_index) & (SUB - 1)
    tile_index = ((lane_index + step_index) & (BLK - 1)) // SUB
    home = (lane_index & (SUB - 1)) == sub_index
    row_all = lax.broadcasted_iota(jnp.int32, (BLK, BLK), 0)
    lane_all = lax.broadcasted_iota(jnp.int32, (BLK, BLK), 1)
    mask_ref[...] = jnp.where(((row_all - lane_all) & (BLK - 1)) < SUB, 1.0, 0.0).astype(LOW)

    weight = weight_ref[...]
    weight_turned = weight.astype(WIDE).T.astype(LOW)

    def project(rows, index):
        proj_ref[index] = jnp.dot(rows, weight, preferred_element_type=WIDE).astype(LOW)
        turned = lax.dot_general(
            weight_turned, rows, (((1,), (1,)), ((), ())), preferred_element_type=WIDE
        ).astype(LOW)
        projt_ref[index] = turned
        return turned.astype(WIDE)

    def skew(row):
        placed = jnp.where(home, spread(row), 0.0)
        placed = placed + pltpu.roll(placed, BLK - 1, 1)
        placed = placed + pltpu.roll(placed, BLK - 2, 1)
        return placed + pltpu.roll(placed, BLK - 4, 1)

    def unskew(tile):
        tile = tile + pltpu.roll(tile, 1, 1)
        tile = tile + pltpu.roll(tile, 2, 1)
        tile = tile + pltpu.roll(tile, 4, 1)
        return jnp.sum(jnp.where(home, tile, 0.0), axis=0, keepdims=True)

    def clear(index):
        grad_src_ref[index] = jnp.zeros((SUB, BLK), WIDE)
        grad_ref[index] = jnp.zeros((head_width, BLK), WIDE)

    def own_table(block, carry):
        rows = own_ref[pl.ds(pl.multiple_of(block * BLK, BLK), BLK), :]
        turned = project(rows, block)
        source = jnp.sum(turned * consts_ref[0], axis=0, keepdims=True)
        target = jnp.sum(turned * consts_ref[1], axis=0, keepdims=True)
        score_ref[block] = skew(source)
        self_score_ref[block] = spread(source)
        dst_score_ref[block] = spread(target)
        clear(block)
        return carry

    lax.fori_loop(0, block_count, own_table, 0)

    def halo_table(block, carry):
        rows = halo_ref[pl.ds(pl.multiple_of(block * BLK, BLK), BLK), :]
        turned = project(rows, block_count + block)
        source = jnp.sum(turned * consts_ref[0], axis=0, keepdims=True)
        slot = (block % PEER_BLOCKS) * BLK + lane_index[:1]
        live = slot < incoming_ref[block // PEER_BLOCKS]
        score_ref[block_count + block] = skew(jnp.where(live, source, -jnp.inf))
        clear(block_count + block)
        return carry

    lax.fori_loop(0, halo_count, halo_table, 0)

    def leaky(values):
        return jnp.maximum(values, 0.2 * values)

    def widen_band(tile, target_ref, turn, pair):
        doubled = jnp.concatenate([tile, tile], 0).astype(LOW)
        for part in range(BLK // (2 * SUB)):
            lead = pair * BLK + part * 2 * SUB
            target_ref[turn, lead : lead + 2 * SUB, :] = (
                doubled * mask_ref[part * 2 * SUB : (part + 1) * 2 * SUB, :]
            )

    def one_block(block, turn):
        nodes = pl.ds(pl.multiple_of(block * BLK, BLK), BLK)
        upstream = cotangent_ref[:, nodes]
        upstream_wide = upstream.astype(WIDE)
        chosen = [local_pairs_ref[block, k] for k in range(local_count)]
        chosen += [remote_pairs_ref[block, k] + block_count for k in range(remote_count)]
        counts = [local_counts_ref[block, k : k + 1, :] for k in range(local_count)]
        counts += [remote_counts_ref[block, k : k + 1, :] for k in range(remote_count)]
        target_score = dst_score_ref[block]
        pre_self = target_score + self_score_ref[block]
        logit_self = leaky(pre_self)
        pre = [target_score + score_ref[index] for index in chosen]
        logits = [
            jnp.where(step_index < spread(count), leaky(value), -jnp.inf)
            for value, count in zip(pre, counts)
        ]
        top = logits[0]
        for logit in logits[1:]:
            top = jnp.maximum(top, logit)
        top = jnp.maximum(spread(jnp.max(top, axis=0, keepdims=True)), logit_self)
        raised = [jnp.exp(logit - top) for logit in logits]
        raised_self = jnp.exp(logit_self - top)
        denom = raised[0]
        for value in raised[1:]:
            denom = denom + value
        denom = spread(jnp.sum(denom, axis=0, keepdims=True)) + raised_self
        scale = 1.0 / denom
        share = [value * scale for value in raised]
        share_self = raised_self * scale
        for pair in range(pair_count):
            widen_band(raised[pair], weights_ref, turn, pair)
            widen_band(share[pair], share_ref, turn, pair)
        sources = jnp.concatenate([projt_ref[index] for index in chosen], 1)
        summed = jnp.dot(sources, weights_ref[turn], preferred_element_type=WIDE)
        self_wide = projt_ref[block].astype(WIDE)
        aggregate = (summed + raised_self[:1] * self_wide) * scale[:1]
        out_ref[:, nodes] = (aggregate + consts_ref[2]).astype(LOW)
        inner = spread(jnp.sum(upstream_wide * aggregate, axis=0, keepdims=True))
        grad_share_self = spread(jnp.sum(upstream_wide * self_wide, axis=0, keepdims=True))
        grad_self = share_self * (grad_share_self - inner) * jnp.where(pre_self > 0, 1.0, 0.2)
        total = None
        for pair in range(pair_count):
            product = jnp.dot(proj_ref[chosen[pair]], upstream, preferred_element_type=WIDE)
            grad_share = product[:SUB]
            for part in range(1, BLK // SUB):
                grad_share = jnp.where(
                    tile_index == part, product[part * SUB : (part + 1) * SUB], grad_share
                )
            grad_pre = share[pair] * (grad_share - inner) * jnp.where(pre[pair] > 0, 1.0, 0.2)
            grad_src_ref[chosen[pair]] += grad_pre
            total = grad_pre if total is None else total + grad_pre
        grad_self_ref[block] = grad_self
        grad_dst_ref[block] = spread(jnp.sum(total, axis=0, keepdims=True)) + grad_self
        grad_sources = lax.dot_general(
            upstream, share_ref[turn], (((1,), (1,)), ((), ())), preferred_element_type=WIDE
        )
        for pair in range(pair_count):
            grad_ref[chosen[pair]] += grad_sources[:, pair * BLK : (pair + 1) * BLK]
        grad_ref[block] += share_self[:1] * upstream_wide

    def one_turn(turn, carry):
        for part in range(SCRATCH_TURNS):
            one_block(turn * SCRATCH_TURNS + part, part)
        return carry

    lax.fori_loop(0, block_count // SCRATCH_TURNS, one_turn, 0)

    def finish(index, rows, own, carry):
        grad_weight, from_src, from_dst = carry
        parts = []
        for part in range(2):
            at = index * 2 + part
            table = at if own else at + block_count
            turned = projt_ref[table].astype(WIDE)
            source = unskew(grad_src_ref[table])
            if own:
                source = source + grad_self_ref[at][:1]
            grad = grad_ref[table] + consts_ref[0] * source
            from_src = from_src + turned * source
            if own:
                target = grad_dst_ref[at][:1]
                grad = grad + consts_ref[1] * target
                from_dst = from_dst + turned * target
            high = grad.astype(LOW)
            low = (grad - high.astype(WIDE)).astype(LOW)
            parts.append(jnp.concatenate([high, low], 0))
        grad_weight = grad_weight + jnp.dot(
            jnp.concatenate(parts, 1), rows, preferred_element_type=WIDE
        )
        return grad_weight, from_src, from_dst

    def finish_own(index, carry):
        rows = own_ref[pl.ds(pl.multiple_of(index * 2 * BLK, BLK), 2 * BLK), :]
        carry = finish(index, rows, True, carry[:3]) + carry[3:]
        nodes = pl.ds(pl.multiple_of(index * 2 * BLK, BLK), 2 * BLK)
        cotangent = cotangent_ref[:, nodes].astype(WIDE)
        return carry[:3] + (carry[3] + cotangent[:, :BLK] + cotangent[:, BLK:],)

    def finish_halo(index, carry):
        rows = halo_ref[pl.ds(pl.multiple_of(index * 2 * BLK, BLK), 2 * BLK), :]
        return finish(index, rows, False, carry)

    zero = jnp.zeros((head_width, BLK), WIDE)
    carry = (jnp.zeros((2 * head_width, own_ref.shape[1]), WIDE), zero, zero, zero)
    carry = lax.fori_loop(0, block_count // 2, finish_own, carry)
    grad_bias = carry[3]
    grad_weight, from_src, from_dst = lax.fori_loop(0, halo_count // 2, finish_halo, carry[:3])
    grad_weight = grad_weight[:head_width] + grad_weight[head_width:]
    lanes = lax.broadcasted_iota(jnp.int32, (head_width, BLK), 1)
    extra = jnp.zeros((head_width, BLK), WIDE)
    for place, value in enumerate((from_src, from_dst, grad_bias)):
        extra = jnp.where(lanes == place, jnp.sum(value, axis=1, keepdims=True), extra)
    shares_ref[...] = jnp.zeros(shares_ref.shape, WIDE)
    peers = shares_ref.shape[0]
    each = head_width // peers
    for peer in range(peers):
        shares_ref[peer, :each, :] = grad_weight[peer * each : (peer + 1) * each]
        shares_ref[peer, each : 2 * each, :] = extra[peer * each : (peer + 1) * each]


def vmem():
    return pl.BlockSpec(memory_space=pltpu.VMEM)


def smem():
    return pl.BlockSpec(memory_space=pltpu.SMEM)


def per_device(
    features,
    weight,
    attention,
    bias,
    cotangent,
    local_pairs,
    local_counts,
    remote_pairs,
    remote_counts,
    send_rows,
    send_counts,
):
    node_count, in_width = features.shape
    head_width = weight.shape[1]
    block_count = node_count // BLK
    peer_count = lax.axis_size("dom")
    capacity = PEER_BLOCKS * BLK
    halo_count = peer_count * PEER_BLOCKS
    slots = peer_count * capacity
    table_count = block_count + halo_count
    pair_rows = (local_pairs.shape[1] + remote_pairs.shape[1]) * BLK
    me = lax.axis_index("dom")
    outgoing_live = lax.dynamic_index_in_dim(send_counts, me, 0, False)
    incoming_live = lax.dynamic_index_in_dim(send_counts, me, 1, False)
    outgoing = pl.pallas_call(
        gather_kernel,
        out_shape=jax.ShapeDtypeStruct((slots, in_width), LOW),
        in_specs=[smem(), smem(), vmem()],
        out_specs=vmem(),
        scratch_shapes=[
            pltpu.VMEM((node_count, in_width), WIDE),
            pltpu.VMEM((slots, in_width), WIDE),
        ],
        compiler_params=pltpu.CompilerParams(vmem_limit_bytes=VMEM_LIMIT),
        name="gather_rows",
    )(send_rows[0], outgoing_live, features)
    halo = lax.all_to_all(
        outgoing.reshape(peer_count, capacity, in_width), "dom", 0, 0, tiled=True
    ).reshape(slots, in_width)
    consts = jnp.broadcast_to(
        jnp.concatenate([attention[:, 0], bias[None]], 0)[:, :, None], (3, head_width, BLK)
    )
    output, shares = pl.pallas_call(
        layer_kernel,
        out_shape=(
            jax.ShapeDtypeStruct((head_width, node_count), LOW),
            jax.ShapeDtypeStruct((peer_count, SUB, in_width), WIDE),
        ),
        in_specs=[smem(), smem(), smem()] + [vmem()] * 7,
        out_specs=(vmem(), vmem()),
        scratch_shapes=[
            pltpu.VMEM((table_count, BLK, head_width), LOW),
            pltpu.VMEM((table_count, head_width, BLK), LOW),
            pltpu.VMEM((table_count, SUB, BLK), WIDE),
            pltpu.VMEM((block_count, SUB, BLK), WIDE),
            pltpu.VMEM((block_count, SUB, BLK), WIDE),
            pltpu.VMEM((table_count, head_width, BLK), WIDE),
            pltpu.VMEM((table_count, SUB, BLK), WIDE),
            pltpu.VMEM((block_count, SUB, BLK), WIDE),
            pltpu.VMEM((block_count, SUB, BLK), WIDE),
            pltpu.VMEM((BLK, BLK), LOW),
            pltpu.VMEM((SCRATCH_TURNS, pair_rows, BLK), LOW),
            pltpu.VMEM((SCRATCH_TURNS, pair_rows, BLK), LOW),
        ],
        compiler_params=pltpu.CompilerParams(vmem_limit_bytes=VMEM_LIMIT),
        name="attention_layer",
    )(
        incoming_live,
        local_pairs,
        remote_pairs,
        features,
        halo,
        weight,
        consts,
        cotangent,
        local_counts,
        remote_counts,
    )
    mine = jnp.sum(lax.all_to_all(shares, "dom", 0, 0, tiled=True), axis=0)
    summed = lax.all_to_all(
        jnp.broadcast_to(mine[None], shares.shape), "dom", 0, 0, tiled=True
    )
    each = head_width // peer_count
    grad_weight = summed[:, :each].reshape(head_width, in_width).T
    extra = summed[:, each : 2 * each, :3].reshape(head_width, 3).T
    return output, grad_weight, extra[:2, None], extra[2]


def solution(mesh):
    return jax.shard_map(
        per_device,
        mesh=mesh,
        in_specs=(
            P("dom", None),
            P(None, "feat"),
            P(None, "feat", None),
            P("feat"),
            P("feat", "dom"),
            P("dom", None),
            P("dom", None, None),
            P("dom", None),
            P("dom", None, None),
            P("dom", None, None),
            P(),
        ),
        out_specs=(P("feat", "dom"), P(None, "feat"), P(None, "feat", None), P("feat")),
        check_vma=False,
    )
```

```python
import jax
import jax.numpy as jnp
from jax import lax
from jax.experimental import pallas as pl
from jax.experimental.pallas import tpu as pltpu
from jax.sharding import PartitionSpec as P

BLK = 128
PEER_BLOCKS = 2
SUB = 8
LOW = jnp.bfloat16
WIDE = jnp.float32
VMEM_LIMIT = 32 * 1024 * 1024
SCRATCH_TURNS = 4
NEAR_GROUP = 4
GATHER_STEP = 32


def gather_kernel(rows_ref, live_ref, features_ref, out_ref, wide_ref, stage_ref):
    node_count = features_ref.shape[0]
    peer_count = live_ref.shape[0]
    capacity = rows_ref.shape[0] // peer_count
    step_count = capacity // GATHER_STEP

    def widen(turn, carry):
        lead = pl.multiple_of(turn * BLK, BLK)
        wide_ref[pl.ds(lead, BLK), :] = features_ref[pl.ds(lead, BLK), :].astype(WIDE)
        return carry

    lax.fori_loop(0, node_count // BLK, widen, 0, unroll=4)

    def one_peer(peer, carry):
        busy = (live_ref[peer] + GATHER_STEP - 1) // GATHER_STEP

        def fetch(step, inner):
            lead = pl.multiple_of(peer * capacity + step * GATHER_STEP, GATHER_STEP)
            for slot in range(GATHER_STEP):
                row = rows_ref[lead + slot]
                stage_ref[pl.ds(lead + slot, 1), :] = wide_ref[pl.ds(row, 1), :]
            return inner

        def blank(step, inner):
            lead = pl.multiple_of(peer * capacity + step * GATHER_STEP, GATHER_STEP)
            stage_ref[pl.ds(lead, GATHER_STEP), :] = jnp.zeros((GATHER_STEP, stage_ref.shape[1]), WIDE)
            return inner

        lax.fori_loop(0, busy, fetch, 0)
        lax.fori_loop(busy, step_count, blank, 0)
        return carry

    lax.fori_loop(0, peer_count, one_peer, 0)

    def narrow(turn, carry):
        lead = pl.multiple_of(turn * BLK, BLK)
        out_ref[pl.ds(lead, BLK), :] = stage_ref[pl.ds(lead, BLK), :].astype(LOW)
        return carry

    lax.fori_loop(0, peer_count * capacity // BLK, narrow, 0, unroll=4)


def spread(row):
    return jnp.broadcast_to(row, (SUB, BLK))


def leaky(values):
    return jnp.maximum(values, 0.2 * values)


def slope_of(values):
    return jnp.where(values > 0, 1.0, 0.2)


def at_block(index, blocks=1):
    return pl.ds(pl.multiple_of(index * blocks * BLK, BLK), blocks * BLK)


def column_sum(values):
    return jnp.sum(values, axis=0, keepdims=True)


def tile_steps():
    sub_index = lax.broadcasted_iota(jnp.int32, (SUB, BLK), 0)
    lane_index = lax.broadcasted_iota(jnp.int32, (SUB, BLK), 1)
    return (sub_index - lane_index) & (SUB - 1), lane_index


def tile_home():
    sub_index = lax.broadcasted_iota(jnp.int32, (SUB, BLK), 0)
    lane_index = lax.broadcasted_iota(jnp.int32, (SUB, BLK), 1)
    return (lane_index & (SUB - 1)) == sub_index


def skew(row):
    placed = jnp.where(tile_home(), spread(row), 0.0)
    placed = placed + pltpu.roll(placed, BLK - 1, 1)
    placed = placed + pltpu.roll(placed, BLK - 2, 1)
    return placed + pltpu.roll(placed, BLK - 4, 1)


def unskew(tile):
    tile = tile + pltpu.roll(tile, 1, 1)
    tile = tile + pltpu.roll(tile, 2, 1)
    tile = tile + pltpu.roll(tile, 4, 1)
    return column_sum(jnp.where(tile_home(), tile, 0.0))


def band_of(product):
    step_index, lane_index = tile_steps()
    tile_index = ((lane_index + step_index) & (BLK - 1)) // SUB
    band = product[:SUB]
    for part in range(1, BLK // SUB):
        band = jnp.where(tile_index == part, product[part * SUB : (part + 1) * SUB], band)
    return band


def project_into(rows, weight, weight_turned, proj_ref, projt_ref, index):
    proj_ref[index] = jnp.dot(rows, weight, preferred_element_type=WIDE).astype(LOW)
    turned = lax.dot_general(
        weight_turned, rows, (((1,), (1,)), ((), ())), preferred_element_type=WIDE
    ).astype(LOW)
    projt_ref[index] = turned
    return turned.astype(WIDE)


def own_kernel(
    local_pairs_ref,
    own_ref,
    weight_ref,
    consts_ref,
    cotangent_ref,
    projt_ref,
    score_ref,
    stats_ref,
    band_ref,
    bias_ref,
    proj_ref,
):
    block_count = own_ref.shape[0] // BLK
    local_count = local_pairs_ref.shape[1]
    weight = weight_ref[...]
    weight_turned = weight.astype(WIDE).T.astype(LOW)

    def one_table(block, grad_bias):
        nodes = at_block(block)
        turned = project_into(own_ref[nodes, :], weight, weight_turned, proj_ref, projt_ref, block)
        source = column_sum(turned * consts_ref[0])
        score_ref[block] = skew(source)
        upstream = cotangent_ref[:, nodes].astype(WIDE)
        stats_ref[block, 0:1, :] = source
        stats_ref[block, 1:2, :] = column_sum(turned * consts_ref[1])
        stats_ref[block, 2:3, :] = column_sum(upstream * turned)
        return grad_bias + upstream

    zero = jnp.zeros((weight.shape[1], BLK), WIDE)
    bias_ref[...] = lax.fori_loop(0, block_count, one_table, zero, unroll=8)

    def one_block(block, carry):
        upstream = cotangent_ref[:, at_block(block)]
        for pair in range(local_count):
            rows = proj_ref[local_pairs_ref[block, pair]]
            band_ref[block, pair] = band_of(jnp.dot(rows, upstream, preferred_element_type=WIDE))
        return carry

    lax.fori_loop(0, block_count, one_block, 0, unroll=2)


def layer_kernel(
    incoming_ref,
    local_pairs_ref,
    remote_pairs_ref,
    own_ref,
    halo_ref,
    weight_ref,
    consts_ref,
    cotangent_ref,
    local_counts_ref,
    remote_counts_ref,
    own_projt_ref,
    own_score_ref,
    stats_ref,
    band_ref,
    bias_ref,
    out_ref,
    shares_ref,
    halo_proj_ref,
    halo_projt_ref,
    halo_score_ref,
    own_grad_ref,
    halo_grad_ref,
    own_src_ref,
    halo_src_ref,
    own_rows_ref,
    mask_ref,
    weights_ref,
    share_ref,
):
    block_count = own_ref.shape[0] // BLK
    halo_count = halo_ref.shape[0] // BLK
    local_count = local_pairs_ref.shape[1]
    remote_count = remote_pairs_ref.shape[1]
    pair_count = local_count + remote_count
    head_width = weight_ref.shape[1]
    step_index, lane_index = tile_steps()
    row_all = lax.broadcasted_iota(jnp.int32, (BLK, BLK), 0)
    lane_all = lax.broadcasted_iota(jnp.int32, (BLK, BLK), 1)
    mask_ref[...] = jnp.where(((row_all - lane_all) & (BLK - 1)) < SUB, 1.0, 0.0).astype(LOW)
    weight = weight_ref[...]
    weight_turned = weight.astype(WIDE).T.astype(LOW)

    own_grad_ref[...] = jnp.zeros(own_grad_ref.shape, WIDE)
    halo_grad_ref[...] = jnp.zeros(halo_grad_ref.shape, WIDE)
    own_src_ref[...] = jnp.zeros(own_src_ref.shape, WIDE)
    halo_src_ref[...] = jnp.zeros(halo_src_ref.shape, WIDE)

    def halo_table(block, carry):
        rows = halo_ref[at_block(block), :]
        turned = project_into(
            rows, weight, weight_turned, halo_proj_ref, halo_projt_ref, block
        )
        source = column_sum(turned * consts_ref[0])
        slot = (block % PEER_BLOCKS) * BLK + lane_index[:1]
        live = slot < incoming_ref[block // PEER_BLOCKS]
        halo_score_ref[block] = skew(jnp.where(live, source, -jnp.inf))
        return carry

    lax.fori_loop(0, halo_count, halo_table, 0, unroll=16)

    def widen_band(tile, target_ref, turn, pair):
        doubled = jnp.concatenate([tile, tile], 0).astype(LOW)
        for part in range(BLK // (2 * SUB)):
            lead = pair * BLK + part * 2 * SUB
            target_ref[turn, lead : lead + 2 * SUB, :] = (
                doubled * mask_ref[part * 2 * SUB : (part + 1) * 2 * SUB, :]
            )

    def one_block(block, turn):
        nodes = at_block(block)
        upstream = cotangent_ref[:, nodes]
        upstream_wide = upstream.astype(WIDE)
        near = [local_pairs_ref[block, k] for k in range(local_count)]
        far = [remote_pairs_ref[block, k] for k in range(remote_count)]
        counts = [local_counts_ref[block, k : k + 1, :] for k in range(local_count)]
        counts += [remote_counts_ref[block, k : k + 1, :] for k in range(remote_count)]
        target_score = spread(stats_ref[block, 1:2, :])
        pre_self = target_score + spread(stats_ref[block, 0:1, :])
        logit_self = leaky(pre_self)
        pre = [target_score + own_score_ref[index] for index in near]
        pre += [target_score + halo_score_ref[index] for index in far]
        logits = [
            jnp.where(step_index < spread(count), leaky(value), -jnp.inf)
            for value, count in zip(pre, counts)
        ]
        top = logits[0]
        for logit in logits[1:]:
            top = jnp.maximum(top, logit)
        top = jnp.maximum(spread(jnp.max(top, axis=0, keepdims=True)), logit_self)
        raised = [jnp.exp(logit - top) for logit in logits]
        raised_self = jnp.exp(logit_self - top)
        denom = raised[0]
        for value in raised[1:]:
            denom = denom + value
        denom = spread(column_sum(denom)) + raised_self
        scale = 1.0 / denom
        share = [value * scale for value in raised]
        share_self = raised_self * scale
        for pair in range(pair_count):
            widen_band(raised[pair], weights_ref, turn, pair)
            widen_band(share[pair], share_ref, turn, pair)
        sources = [own_projt_ref[index] for index in near]
        sources = jnp.concatenate(sources + [halo_projt_ref[index] for index in far], 1)
        summed = jnp.dot(sources, weights_ref[turn], preferred_element_type=WIDE)
        self_wide = own_projt_ref[block].astype(WIDE)
        aggregate = (summed + raised_self[:1] * self_wide) * scale[:1]
        out_ref[:, nodes] = (aggregate + consts_ref[2]).astype(LOW)
        inner = spread(column_sum(upstream_wide * aggregate))
        grad_self = share_self * (spread(stats_ref[block, 2:3, :]) - inner) * slope_of(pre_self)
        total = None
        for pair in range(pair_count):
            if pair < local_count:
                grad_share = band_ref[block, pair]
            else:
                rows = halo_proj_ref[far[pair - local_count]]
                grad_share = band_of(jnp.dot(rows, upstream, preferred_element_type=WIDE))
            grad_pre = share[pair] * (grad_share - inner) * slope_of(pre[pair])
            if pair < local_count:
                own_src_ref[near[pair]] += grad_pre
            else:
                halo_src_ref[far[pair - local_count]] += grad_pre
            total = grad_pre if total is None else total + grad_pre
        own_rows_ref[block, 0:1, :] = grad_self[:1]
        own_rows_ref[block, 1:2, :] = column_sum(total) + grad_self[:1]
        grad_sources = lax.dot_general(
            upstream, share_ref[turn], (((1,), (1,)), ((), ())), preferred_element_type=WIDE
        )
        for pair in range(pair_count):
            if pair < local_count:
                own_grad_ref[near[pair]] += grad_sources[:, pair * BLK : (pair + 1) * BLK]
            else:
                index = far[pair - local_count]
                halo_grad_ref[index] += grad_sources[:, pair * BLK : (pair + 1) * BLK]
        own_grad_ref[block] += share_self[:1] * upstream_wide

    def one_turn(turn, carry):
        for part in range(SCRATCH_TURNS):
            one_block(turn * SCRATCH_TURNS + part, part)
        return carry

    lax.fori_loop(0, block_count // SCRATCH_TURNS, one_turn, 0)

    def finish(index, rows, own, carry):
        grad_weight, from_src, from_dst = carry
        parts = []
        for part in range(2):
            at = index * 2 + part
            if own:
                turned = own_projt_ref[at].astype(WIDE)
                source = unskew(own_src_ref[at]) + own_rows_ref[at, 0:1, :]
                target = own_rows_ref[at, 1:2, :]
                grad = own_grad_ref[at] + consts_ref[0] * source + consts_ref[1] * target
                from_dst = from_dst + turned * target
            else:
                turned = halo_projt_ref[at].astype(WIDE)
                source = unskew(halo_src_ref[at])
                grad = halo_grad_ref[at] + consts_ref[0] * source
            from_src = from_src + turned * source
            high = grad.astype(LOW)
            low = (grad - high.astype(WIDE)).astype(LOW)
            parts.append(jnp.concatenate([high, low], 0))
        grad_weight = grad_weight + jnp.dot(
            jnp.concatenate(parts, 1), rows, preferred_element_type=WIDE
        )
        return grad_weight, from_src, from_dst

    def finish_own(index, carry):
        return finish(index, own_ref[at_block(index, 2), :], True, carry)

    def finish_halo(index, carry):
        return finish(index, halo_ref[at_block(index, 2), :], False, carry)

    zero = jnp.zeros((head_width, BLK), WIDE)
    carry = (jnp.zeros((2 * head_width, own_ref.shape[1]), WIDE), zero, zero)
    carry = lax.fori_loop(0, block_count // 2, finish_own, carry, unroll=8)
    carry = lax.fori_loop(0, halo_count // 2, finish_halo, carry, unroll=8)
    grad_weight, from_src, from_dst = carry
    grad_weight = grad_weight[:head_width] + grad_weight[head_width:]
    lanes = lax.broadcasted_iota(jnp.int32, (head_width, BLK), 1)
    extra = jnp.zeros((head_width, BLK), WIDE)
    for place, value in enumerate((from_src, from_dst, bias_ref[...])):
        extra = jnp.where(lanes == place, jnp.sum(value, axis=1, keepdims=True), extra)
    extra = jnp.concatenate([extra, jnp.zeros((BLK - head_width, BLK), WIDE)], 0).T
    for copy in range(shares_ref.shape[0]):
        shares_ref[copy, :head_width, :] = grad_weight
        shares_ref[copy, head_width:, :] = extra[:SUB]


def relay_kernel(parts_ref, out_ref):
    total = parts_ref[0]
    for part in range(1, parts_ref.shape[0]):
        total = total + parts_ref[part]
    for copy in range(out_ref.shape[0]):
        out_ref[copy] = total


def last_kernel(parts_ref, weight_ref, attention_ref, bias_ref):
    total = parts_ref[0]
    for part in range(1, parts_ref.shape[0]):
        total = total + parts_ref[part]
    head_width = weight_ref.shape[1]
    weight_ref[...] = total[:head_width].T
    attention_ref[0] = total[head_width : head_width + 1, :head_width]
    attention_ref[1] = total[head_width + 1 : head_width + 2, :head_width]
    bias_ref[...] = total[head_width + 2 : head_width + 3, :head_width]


def vmem():
    return pl.BlockSpec(memory_space=pltpu.VMEM)


def smem():
    return pl.BlockSpec(memory_space=pltpu.SMEM)


def gather_rows(rows, live, features):
    slots = rows.shape[0]
    node_count, in_width = features.shape
    return pl.pallas_call(
        gather_kernel,
        out_shape=jax.ShapeDtypeStruct((slots, in_width), LOW),
        in_specs=[smem(), smem(), vmem()],
        out_specs=vmem(),
        scratch_shapes=[
            pltpu.VMEM((node_count, in_width), WIDE),
            pltpu.VMEM((slots, in_width), WIDE),
        ],
        compiler_params=pltpu.CompilerParams(vmem_limit_bytes=VMEM_LIMIT),
        name="gather_rows",
    )(rows, live, features)


def own_part(*operands):
    local_pairs, features, weight = operands[:3]
    head_width = weight.shape[1]
    block_count = features.shape[0] // BLK
    local_count = local_pairs.shape[1]
    tiles = jax.ShapeDtypeStruct((block_count, SUB, BLK), WIDE)
    return pl.pallas_call(
        own_kernel,
        out_shape=(
            jax.ShapeDtypeStruct((block_count, head_width, BLK), LOW),
            tiles,
            tiles,
            jax.ShapeDtypeStruct((block_count, local_count, SUB, BLK), WIDE),
            jax.ShapeDtypeStruct((head_width, BLK), WIDE),
        ),
        in_specs=[smem()] + [vmem()] * 4,
        out_specs=(vmem(),) * 5,
        scratch_shapes=[pltpu.VMEM((block_count, BLK, head_width), LOW)],
        compiler_params=pltpu.CompilerParams(vmem_limit_bytes=VMEM_LIMIT),
        cost_estimate=pl.CostEstimate(flops=10**10, bytes_accessed=8 * 10**6, transcendentals=0),
        name="own_part",
    )(*operands)


def attention_layer(*operands):
    local_pairs, remote_pairs, features, halo, weight = operands[1:6]
    node_count, in_width = features.shape
    head_width = weight.shape[1]
    block_count = node_count // BLK
    halo_count = halo.shape[0] // BLK
    pair_rows = (local_pairs.shape[1] + remote_pairs.shape[1]) * BLK
    return pl.pallas_call(
        layer_kernel,
        out_shape=(
            jax.ShapeDtypeStruct((head_width, node_count), LOW),
            jax.ShapeDtypeStruct((NEAR_GROUP, head_width + SUB, in_width), WIDE),
        ),
        in_specs=[smem(), smem(), smem()] + [vmem()] * 12,
        out_specs=(vmem(), vmem()),
        scratch_shapes=[
            pltpu.VMEM((halo_count, BLK, head_width), LOW),
            pltpu.VMEM((halo_count, head_width, BLK), LOW),
            pltpu.VMEM((halo_count, SUB, BLK), WIDE),
            pltpu.VMEM((block_count, head_width, BLK), WIDE),
            pltpu.VMEM((halo_count, head_width, BLK), WIDE),
            pltpu.VMEM((block_count, SUB, BLK), WIDE),
            pltpu.VMEM((halo_count, SUB, BLK), WIDE),
            pltpu.VMEM((block_count, SUB, BLK), WIDE),
            pltpu.VMEM((BLK, BLK), LOW),
            pltpu.VMEM((SCRATCH_TURNS, pair_rows, BLK), LOW),
            pltpu.VMEM((SCRATCH_TURNS, pair_rows, BLK), LOW),
        ],
        compiler_params=pltpu.CompilerParams(vmem_limit_bytes=VMEM_LIMIT),
        cost_estimate=pl.CostEstimate(flops=10**10, bytes_accessed=10**7, transcendentals=0),
        name="attention_layer",
    )(*operands)


def per_device(
    features,
    weight,
    attention,
    bias,
    cotangent,
    local_pairs,
    local_counts,
    remote_pairs,
    remote_counts,
    send_rows,
    send_counts,
):
    node_count, in_width = features.shape
    head_width = weight.shape[1]
    peer_count = lax.axis_size("dom")
    capacity = PEER_BLOCKS * BLK
    slots = peer_count * capacity
    me = lax.axis_index("dom")
    outgoing_live = lax.dynamic_index_in_dim(send_counts, me, 0, False)
    incoming_live = lax.dynamic_index_in_dim(send_counts, me, 1, False)
    outgoing = gather_rows(send_rows.reshape(-1), outgoing_live, features)
    halo = lax.all_to_all(
        outgoing.reshape(peer_count, capacity, in_width), "dom", 0, 0, tiled=True
    ).reshape(slots, in_width)
    consts = jnp.broadcast_to(
        jnp.concatenate([attention[:, 0], bias[None]], 0)[:, :, None], (3, head_width, BLK)
    )
    own = own_part(local_pairs, features, weight, consts, cotangent)
    output, shares = attention_layer(
        incoming_live,
        local_pairs,
        remote_pairs,
        features,
        halo,
        weight,
        consts,
        cotangent,
        local_counts,
        remote_counts,
        *own,
    )
    near = [
        [base + step for step in range(NEAR_GROUP)] for base in range(0, peer_count, NEAR_GROUP)
    ]
    far = [list(range(base, peer_count, NEAR_GROUP)) for base in range(NEAR_GROUP)]
    shares = exchange(shares, near)
    relayed = pl.pallas_call(
        relay_kernel,
        out_shape=jax.ShapeDtypeStruct((peer_count // NEAR_GROUP,) + shares.shape[1:], WIDE),
        in_specs=[vmem()],
        out_specs=vmem(),
        name="relay_sums",
    )(shares)
    grad_weight, grad_attention, grad_bias = pl.pallas_call(
        last_kernel,
        out_shape=(
            jax.ShapeDtypeStruct((in_width, head_width), WIDE),
            jax.ShapeDtypeStruct((2, 1, head_width), WIDE),
            jax.ShapeDtypeStruct((1, head_width), WIDE),
        ),
        in_specs=[vmem()],
        out_specs=(vmem(), vmem(), vmem()),
        name="last_sums",
    )(exchange(relayed, far))
    return output, grad_weight, grad_attention, grad_bias[0]


def exchange(values, groups):
    return lax.all_to_all(values, "dom", 0, 0, tiled=True, axis_index_groups=groups)


def solution(mesh):
    return jax.shard_map(
        per_device,
        mesh=mesh,
        in_specs=(
            P("dom", None),
            P(None, "feat"),
            P(None, "feat", None),
            P("feat"),
            P("feat", "dom"),
            P("dom", None),
            P("dom", None, None),
            P("dom", None),
            P("dom", None, None),
            P("dom", None, None),
            P(),
        ),
        out_specs=(P("feat", "dom"), P(None, "feat"), P(None, "feat", None), P("feat")),
        check_vma=False,
    )
```

```python
import jax
import jax.numpy as jnp
from jax import lax
from jax.experimental import pallas as pl
from jax.experimental.pallas import tpu as pltpu
from jax.sharding import PartitionSpec as P

BLK = 128
PEER_BLOCKS = 2
SUB = 8
LOW = jnp.bfloat16
WIDE = jnp.float32
VMEM_LIMIT = 32 * 1024 * 1024
OWN_LIMIT = 56 * 1024 * 1024
LAYER_LIMIT = 58 * 1024 * 1024
TURN_BLOCKS = 8
WEIGHT_GROUP = 8
SHARE_GROUP = 2
GATHER_STEP = 32


def gather_kernel(rows_ref, live_ref, features_ref, out_ref, wide_ref, stage_ref):
    node_count = features_ref.shape[0]
    peer_count = live_ref.shape[0]
    capacity = rows_ref.shape[0] // peer_count
    step_count = capacity // GATHER_STEP

    def widen(turn, carry):
        lead = pl.multiple_of(turn * BLK, BLK)
        wide_ref[pl.ds(lead, BLK), :] = features_ref[pl.ds(lead, BLK), :].astype(WIDE)
        return carry

    lax.fori_loop(0, node_count // BLK, widen, 0, unroll=4)

    def one_peer(peer, carry):
        busy = (live_ref[peer] + GATHER_STEP - 1) // GATHER_STEP

        def fetch(step, inner):
            lead = pl.multiple_of(peer * capacity + step * GATHER_STEP, GATHER_STEP)
            for slot in range(GATHER_STEP):
                row = rows_ref[lead + slot]
                stage_ref[pl.ds(lead + slot, 1), :] = wide_ref[pl.ds(row, 1), :]
            return inner

        def blank(step, inner):
            lead = pl.multiple_of(peer * capacity + step * GATHER_STEP, GATHER_STEP)
            stage_ref[pl.ds(lead, GATHER_STEP), :] = jnp.zeros((GATHER_STEP, stage_ref.shape[1]), WIDE)
            return inner

        lax.fori_loop(0, busy, fetch, 0)
        lax.fori_loop(busy, step_count, blank, 0)
        return carry

    lax.fori_loop(0, peer_count, one_peer, 0)

    def narrow(turn, carry):
        lead = pl.multiple_of(turn * BLK, BLK)
        out_ref[pl.ds(lead, BLK), :] = stage_ref[pl.ds(lead, BLK), :].astype(LOW)
        return carry

    lax.fori_loop(0, peer_count * capacity // BLK, narrow, 0, unroll=4)


def spread(row):
    return jnp.broadcast_to(row, (SUB, BLK))


def leaky(values):
    return jnp.maximum(values, 0.2 * values)


def slope_of(values):
    return jnp.where(values > 0, 1.0, 0.2)


def at_block(index, blocks=1):
    return pl.ds(pl.multiple_of(index * blocks * BLK, BLK), blocks * BLK)


def column_sum(values):
    return jnp.sum(values, axis=0, keepdims=True)


def tile_steps():
    sub_index = lax.broadcasted_iota(jnp.int32, (SUB, BLK), 0)
    lane_index = lax.broadcasted_iota(jnp.int32, (SUB, BLK), 1)
    return (sub_index - lane_index) & (SUB - 1), lane_index


def tile_home():
    sub_index = lax.broadcasted_iota(jnp.int32, (SUB, BLK), 0)
    lane_index = lax.broadcasted_iota(jnp.int32, (SUB, BLK), 1)
    return (lane_index & (SUB - 1)) == sub_index


def skew(row):
    placed = jnp.where(tile_home(), spread(row), 0.0)
    placed = placed + pltpu.roll(placed, BLK - 1, 1)
    placed = placed + pltpu.roll(placed, BLK - 2, 1)
    return placed + pltpu.roll(placed, BLK - 4, 1)


def unskew(tile):
    tile = tile + pltpu.roll(tile, 1, 1)
    tile = tile + pltpu.roll(tile, 2, 1)
    tile = tile + pltpu.roll(tile, 4, 1)
    return column_sum(jnp.where(tile_home(), tile, 0.0))


def band_of(product):
    step_index, lane_index = tile_steps()
    tile_index = ((lane_index + step_index) & (BLK - 1)) // SUB
    band = product[:SUB]
    for part in range(1, BLK // SUB):
        band = jnp.where(tile_index == part, product[part * SUB : (part + 1) * SUB], band)
    return band


def project_into(rows, weight, weight_turned, proj_ref, projt_ref, index):
    proj_ref[index] = jnp.dot(rows, weight, preferred_element_type=WIDE).astype(LOW)
    turned = lax.dot_general(
        weight_turned, rows, (((1,), (1,)), ((), ())), preferred_element_type=WIDE
    ).astype(LOW)
    projt_ref[index] = turned
    return turned.astype(WIDE)


def own_kernel(
    local_pairs_ref,
    own_ref,
    weight_ref,
    consts_ref,
    cotangent_ref,
    projt_ref,
    score_ref,
    stats_ref,
    band_ref,
    bias_ref,
    proj_ref,
):
    block_count = own_ref.shape[0] // BLK
    local_count = local_pairs_ref.shape[1]
    weight = weight_ref[...]
    weight_turned = weight.astype(WIDE).T.astype(LOW)

    def one_table(block, grad_bias):
        nodes = at_block(block)
        turned = project_into(own_ref[nodes, :], weight, weight_turned, proj_ref, projt_ref, block)
        source = column_sum(turned * consts_ref[0])
        score_ref[block] = skew(source)
        upstream = cotangent_ref[:, nodes].astype(WIDE)
        stats_ref[block, 0:1, :] = source
        stats_ref[block, 1:2, :] = column_sum(turned * consts_ref[1])
        stats_ref[block, 2:3, :] = column_sum(upstream * turned)
        return grad_bias + upstream

    zero = jnp.zeros((weight.shape[1], BLK), WIDE)
    bias_ref[...] = lax.fori_loop(0, block_count, one_table, zero, unroll=8)

    def one_block(block, carry):
        upstream = cotangent_ref[:, at_block(block)]
        for pair in range(local_count):
            rows = proj_ref[local_pairs_ref[block, pair]]
            band_ref[block, pair] = band_of(jnp.dot(rows, upstream, preferred_element_type=WIDE))
        return carry

    lax.fori_loop(0, block_count, one_block, 0, unroll=2)


def layer_kernel(
    incoming_ref,
    local_pairs_ref,
    remote_pairs_ref,
    weight_ref,
    consts_ref,
    bias_ref,
    halo_hbm,
    own_projt_hbm,
    own_score_hbm,
    stats_hbm,
    cotangent_hbm,
    local_counts_hbm,
    remote_counts_hbm,
    band_hbm,
    own_hbm,
    out_hbm,
    shares_ref,
    halo_proj_ref,
    halo_projt_ref,
    halo_score_ref,
    own_grad_ref,
    halo_grad_ref,
    own_src_ref,
    halo_src_ref,
    own_rows_ref,
    mask_ref,
    halo_ref,
    own_projt_ref,
    own_score_ref,
    stats_ref,
    cotangent_ref,
    local_counts_ref,
    remote_counts_ref,
    band_ref,
    own_ref,
    out_ref,
    copy_sem,
):
    fetches = []
    for place, (source, target) in enumerate(
        (
            (halo_hbm, halo_ref),
            (own_projt_hbm, own_projt_ref),
            (own_score_hbm, own_score_ref),
            (stats_hbm, stats_ref),
            (cotangent_hbm, cotangent_ref),
            (local_counts_hbm, local_counts_ref),
            (remote_counts_hbm, remote_counts_ref),
            (band_hbm, band_ref),
            (own_hbm, own_ref),
        )
    ):
        fetches.append(pltpu.make_async_copy(source, target, copy_sem.at[place]))
    for fetch in fetches:
        fetch.start()
    block_count = own_ref.shape[0] // BLK
    halo_count = halo_ref.shape[0] // BLK
    local_count = local_pairs_ref.shape[1]
    remote_count = remote_pairs_ref.shape[1]
    pair_count = local_count + remote_count
    head_width = weight_ref.shape[1]
    step_index, lane_index = tile_steps()
    row_all = lax.broadcasted_iota(jnp.int32, (BLK, BLK), 0)
    lane_all = lax.broadcasted_iota(jnp.int32, (BLK, BLK), 1)
    mask_ref[...] = jnp.where(((row_all - lane_all) & (BLK - 1)) < SUB, 1.0, 0.0).astype(LOW)
    weight = weight_ref[...]
    weight_turned = weight.astype(WIDE).T.astype(LOW)

    own_grad_ref[...] = jnp.zeros(own_grad_ref.shape, WIDE)
    halo_grad_ref[...] = jnp.zeros(halo_grad_ref.shape, WIDE)
    own_src_ref[...] = jnp.zeros(own_src_ref.shape, WIDE)
    halo_src_ref[...] = jnp.zeros(halo_src_ref.shape, WIDE)

    fetches[0].wait()

    def halo_table(block, carry):
        rows = halo_ref[at_block(block), :]
        turned = project_into(
            rows, weight, weight_turned, halo_proj_ref, halo_projt_ref, block
        )
        source = column_sum(turned * consts_ref[0])
        slot = (block % PEER_BLOCKS) * BLK + lane_index[:1]
        live = slot < incoming_ref[block // PEER_BLOCKS]
        halo_score_ref[block] = skew(jnp.where(live, source, -jnp.inf))
        return carry

    lax.fori_loop(0, halo_count, halo_table, 0, unroll=16)

    def band_values(tiles):
        parts = []
        for tile in tiles:
            doubled = jnp.concatenate([tile, tile], 0).astype(LOW)
            for lead in range(0, BLK, 2 * SUB):
                parts.append(doubled * mask_ref[lead : lead + 2 * SUB, :])
        return jnp.concatenate(parts, 0)

    def one_block(block):
        nodes = at_block(block)
        upstream = cotangent_ref[:, nodes]
        upstream_wide = upstream.astype(WIDE)
        near = [local_pairs_ref[block, k] for k in range(local_count)]
        far = [remote_pairs_ref[block, k] for k in range(remote_count)]
        counts = [local_counts_ref[block, k : k + 1, :] for k in range(local_count)]
        counts += [remote_counts_ref[block, k : k + 1, :] for k in range(remote_count)]
        target_score = spread(stats_ref[block, 1:2, :])
        pre_self = target_score + spread(stats_ref[block, 0:1, :])
        logit_self = leaky(pre_self)
        pre = [target_score + own_score_ref[index] for index in near]
        pre += [target_score + halo_score_ref[index] for index in far]
        logits = [
            jnp.where(step_index < spread(count), leaky(value), -jnp.inf)
            for value, count in zip(pre, counts)
        ]
        top = logits[0]
        for logit in logits[1:]:
            top = jnp.maximum(top, logit)
        top = jnp.maximum(spread(jnp.max(top, axis=0, keepdims=True)), logit_self)
        raised = [jnp.exp(logit - top) for logit in logits]
        raised_self = jnp.exp(logit_self - top)
        denom = raised[0]
        for value in raised[1:]:
            denom = denom + value
        denom = spread(column_sum(denom)) + raised_self
        scale = 1.0 / denom
        share = [value * scale for value in raised]
        share_self = raised_self * scale
        sources = [own_projt_ref[index] for index in near]
        sources += [halo_projt_ref[index] for index in far]
        summed = None
        for lead in range(0, pair_count, WEIGHT_GROUP):
            group = slice(lead, lead + WEIGHT_GROUP)
            part = jnp.dot(
                jnp.concatenate(sources[group], 1),
                band_values(raised[group]),
                preferred_element_type=WIDE,
            )
            summed = part if summed is None else summed + part
        self_wide = own_projt_ref[block].astype(WIDE)
        aggregate = (summed + raised_self[:1] * self_wide) * scale[:1]
        out_ref[:, nodes] = (aggregate + consts_ref[2]).astype(LOW)
        inner = spread(column_sum(upstream_wide * aggregate))
        grad_self = share_self * (spread(stats_ref[block, 2:3, :]) - inner) * slope_of(pre_self)
        total = None
        for pair in range(pair_count):
            if pair < local_count:
                grad_share = band_ref[block, pair]
            else:
                rows = halo_proj_ref[far[pair - local_count]]
                grad_share = band_of(jnp.dot(rows, upstream, preferred_element_type=WIDE))
            grad_pre = share[pair] * (grad_share - inner) * slope_of(pre[pair])
            if pair < local_count:
                own_src_ref[near[pair]] += grad_pre
            else:
                halo_src_ref[far[pair - local_count]] += grad_pre
            total = grad_pre if total is None else total + grad_pre
        own_rows_ref[block, 0:1, :] = grad_self[:1]
        own_rows_ref[block, 1:2, :] = column_sum(total) + grad_self[:1]
        for lead in range(0, pair_count, SHARE_GROUP):
            grad_sources = lax.dot_general(
                upstream,
                band_values(share[lead : lead + SHARE_GROUP]),
                (((1,), (1,)), ((), ())),
                preferred_element_type=WIDE,
            )
            for pair in range(lead, min(lead + SHARE_GROUP, pair_count)):
                grad = grad_sources[:, (pair - lead) * BLK : (pair - lead + 1) * BLK]
                if pair < local_count:
                    own_grad_ref[near[pair]] += grad
                else:
                    halo_grad_ref[far[pair - local_count]] += grad
        own_grad_ref[block] += share_self[:1] * upstream_wide

    def one_turn(turn, carry):
        for part in range(TURN_BLOCKS):
            one_block(turn * TURN_BLOCKS + part)
        return carry

    for fetch in fetches[1:-1]:
        fetch.wait()
    lax.fori_loop(0, block_count // TURN_BLOCKS, one_turn, 0)
    store = pltpu.make_async_copy(out_ref, out_hbm, copy_sem.at[len(fetches)])
    store.start()
    fetches[-1].wait()

    def finish(index, rows, own, carry):
        grad_weight, from_src, from_dst = carry
        parts = []
        for part in range(2):
            at = index * 2 + part
            if own:
                turned = own_projt_ref[at].astype(WIDE)
                source = unskew(own_src_ref[at]) + own_rows_ref[at, 0:1, :]
                target = own_rows_ref[at, 1:2, :]
                grad = own_grad_ref[at] + consts_ref[0] * source + consts_ref[1] * target
                from_dst = from_dst + turned * target
            else:
                turned = halo_projt_ref[at].astype(WIDE)
                source = unskew(halo_src_ref[at])
                grad = halo_grad_ref[at] + consts_ref[0] * source
            from_src = from_src + turned * source
            high = grad.astype(LOW)
            low = (grad - high.astype(WIDE)).astype(LOW)
            parts.append(jnp.concatenate([high, low], 0))
        grad_weight = grad_weight + jnp.dot(
            jnp.concatenate(parts, 1), rows, preferred_element_type=WIDE
        )
        return grad_weight, from_src, from_dst

    def finish_own(index, carry):
        return finish(index, own_ref[at_block(index, 2), :], True, carry)

    def finish_halo(index, carry):
        return finish(index, halo_ref[at_block(index, 2), :], False, carry)

    zero = jnp.zeros((head_width, BLK), WIDE)
    carry = (jnp.zeros((2 * head_width, own_ref.shape[1]), WIDE), zero, zero)
    carry = lax.fori_loop(0, block_count // 2, finish_own, carry, unroll=8)
    carry = lax.fori_loop(0, halo_count // 2, finish_halo, carry, unroll=8)
    grad_weight, from_src, from_dst = carry
    grad_weight = grad_weight[:head_width] + grad_weight[head_width:]
    lanes = lax.broadcasted_iota(jnp.int32, (head_width, BLK), 1)
    extra = jnp.zeros((head_width, BLK), WIDE)
    for place, value in enumerate((from_src, from_dst, bias_ref[...])):
        extra = jnp.where(lanes == place, jnp.sum(value, axis=1, keepdims=True), extra)
    extra = jnp.concatenate([extra, jnp.zeros((BLK - head_width, BLK), WIDE)], 0).T
    for copy in range(shares_ref.shape[0]):
        shares_ref[copy, :head_width, :] = grad_weight
        shares_ref[copy, head_width:, :] = extra[:SUB]
    store.wait()


def last_kernel(parts_ref, weight_ref, attention_ref, bias_ref):
    total = parts_ref[0]
    for part in range(1, parts_ref.shape[0]):
        total = total + parts_ref[part]
    head_width = weight_ref.shape[0]
    weight_ref[...] = total[:head_width]
    attention_ref[0] = total[head_width : head_width + 1, :head_width]
    attention_ref[1] = total[head_width + 1 : head_width + 2, :head_width]
    bias_ref[...] = total[head_width + 2 : head_width + 3, :head_width]


def vmem():
    return pl.BlockSpec(memory_space=pltpu.VMEM)


def anywhere():
    return pl.BlockSpec(memory_space=pl.ANY)


def smem():
    return pl.BlockSpec(memory_space=pltpu.SMEM)


def gather_rows(rows, live, features):
    slots = rows.shape[0]
    node_count, in_width = features.shape
    return pl.pallas_call(
        gather_kernel,
        out_shape=jax.ShapeDtypeStruct((slots, in_width), LOW),
        in_specs=[smem(), smem(), vmem()],
        out_specs=vmem(),
        scratch_shapes=[
            pltpu.VMEM((node_count, in_width), WIDE),
            pltpu.VMEM((slots, in_width), WIDE),
        ],
        compiler_params=pltpu.CompilerParams(vmem_limit_bytes=VMEM_LIMIT),
        name="gather_rows",
    )(rows, live, features)


def own_part(*operands):
    local_pairs, features, weight = operands[:3]
    head_width = weight.shape[1]
    block_count = features.shape[0] // BLK
    local_count = local_pairs.shape[1]
    tiles = jax.ShapeDtypeStruct((block_count, SUB, BLK), WIDE)
    return pl.pallas_call(
        own_kernel,
        out_shape=(
            jax.ShapeDtypeStruct((block_count, head_width, BLK), LOW),
            tiles,
            tiles,
            jax.ShapeDtypeStruct((block_count, local_count, SUB, BLK), WIDE),
            jax.ShapeDtypeStruct((head_width, BLK), WIDE),
        ),
        in_specs=[smem()] + [vmem()] * 4,
        out_specs=(vmem(),) * 5,
        scratch_shapes=[pltpu.VMEM((block_count, BLK, head_width), LOW)],
        compiler_params=pltpu.CompilerParams(vmem_limit_bytes=OWN_LIMIT),
        cost_estimate=pl.CostEstimate(flops=10**10, bytes_accessed=8 * 10**6, transcendentals=0),
        name="own_part",
    )(*operands)


def attention_layer(*operands):
    incoming, local_pairs, remote_pairs, weight = operands[:4]
    streamed = operands[6:]
    halo, cotangent = streamed[0], streamed[4]
    peer_count = incoming.shape[0]
    in_width = halo.shape[1]
    head_width, node_count = cotangent.shape
    block_count = node_count // BLK
    halo_count = halo.shape[0] // BLK
    return pl.pallas_call(
        layer_kernel,
        out_shape=(
            jax.ShapeDtypeStruct((head_width, node_count), LOW),
            jax.ShapeDtypeStruct((peer_count, head_width + SUB, in_width), WIDE),
        ),
        in_specs=[smem()] * 3 + [vmem()] * 3 + [anywhere()] * len(streamed),
        out_specs=(anywhere(), vmem()),
        scratch_shapes=[
            pltpu.VMEM((halo_count, BLK, head_width), LOW),
            pltpu.VMEM((halo_count, head_width, BLK), LOW),
            pltpu.VMEM((halo_count, SUB, BLK), WIDE),
            pltpu.VMEM((block_count, head_width, BLK), WIDE),
            pltpu.VMEM((halo_count, head_width, BLK), WIDE),
            pltpu.VMEM((block_count, SUB, BLK), WIDE),
            pltpu.VMEM((halo_count, SUB, BLK), WIDE),
            pltpu.VMEM((block_count, SUB, BLK), WIDE),
            pltpu.VMEM((BLK, BLK), LOW),
        ]
        + [pltpu.VMEM(value.shape, value.dtype) for value in streamed]
        + [
            pltpu.VMEM((head_width, node_count), LOW),
            pltpu.SemaphoreType.DMA((len(streamed) + 1,)),
        ],
        compiler_params=pltpu.CompilerParams(vmem_limit_bytes=LAYER_LIMIT),
        cost_estimate=pl.CostEstimate(flops=10**10, bytes_accessed=10**7, transcendentals=0),
        name="attention_layer",
    )(*operands)


def per_device(
    features,
    weight,
    attention,
    bias,
    cotangent,
    local_pairs,
    local_counts,
    remote_pairs,
    remote_counts,
    send_rows,
    send_counts,
):
    node_count, in_width = features.shape
    head_width = weight.shape[1]
    peer_count = lax.axis_size("dom")
    capacity = PEER_BLOCKS * BLK
    slots = peer_count * capacity
    me = lax.axis_index("dom")
    outgoing_live = lax.dynamic_index_in_dim(send_counts, me, 0, False)
    incoming_live = lax.dynamic_index_in_dim(send_counts, me, 1, False)
    outgoing = gather_rows(send_rows.reshape(-1), outgoing_live, features)
    halo = lax.all_to_all(
        outgoing.reshape(peer_count, capacity, in_width), "dom", 0, 0, tiled=True
    ).reshape(slots, in_width)
    consts = jnp.broadcast_to(
        jnp.concatenate([attention[:, 0], bias[None]], 0)[:, :, None], (3, head_width, BLK)
    )
    projt, score, stats, band, grad_bias = own_part(
        local_pairs, features, weight, consts, cotangent
    )
    output, shares = attention_layer(
        incoming_live,
        local_pairs,
        remote_pairs,
        weight,
        consts,
        grad_bias,
        halo,
        projt,
        score,
        stats,
        cotangent,
        local_counts,
        remote_counts,
        band,
        features,
    )
    gathered = lax.all_to_all(shares, "dom", 0, 0, tiled=True)
    grad_weight, grad_attention, grad_bias = pl.pallas_call(
        last_kernel,
        out_shape=(
            jax.ShapeDtypeStruct((head_width, in_width), WIDE),
            jax.ShapeDtypeStruct((2, 1, head_width), WIDE),
            jax.ShapeDtypeStruct((1, head_width), WIDE),
        ),
        in_specs=[vmem()],
        out_specs=(vmem(), vmem(), vmem()),
        name="last_sums",
    )(gathered)
    return output, grad_weight.T, grad_attention, grad_bias[0]


def solution(mesh):
    return jax.shard_map(
        per_device,
        mesh=mesh,
        in_specs=(
            P("dom", None),
            P(None, "feat"),
            P(None, "feat", None),
            P("feat"),
            P("feat", "dom"),
            P("dom", None),
            P("dom", None, None),
            P("dom", None),
            P("dom", None, None),
            P("dom", None, None),
            P(),
        ),
        out_specs=(P("feat", "dom"), P(None, "feat"), P(None, "feat", None), P("feat")),
        check_vma=False,
    )
```

```python
import jax
import jax.numpy as jnp
from jax import lax
from jax.experimental import pallas as pl
from jax.experimental.pallas import tpu as pltpu
from jax.sharding import PartitionSpec as P

BLK = 128
PEER_BLOCKS = 2
SUB = 8
LOW = jnp.bfloat16
WIDE = jnp.float32
VMEM_LIMIT = 32 * 1024 * 1024
OWN_LIMIT = 62 * 1024 * 1024
SMALL_LIMIT = 4 * 1024 * 1024
LAYER_LIMIT = 60 * 1024 * 1024
TURN_BLOCKS = 8
WEIGHT_GROUP = 8
SHARE_GROUP = 2
GATHER_STEP = 32


def gather_kernel(rows_ref, live_ref, features_ref, out_ref, wide_ref, stage_ref):
    node_count = features_ref.shape[0]
    peer_count = live_ref.shape[0]
    capacity = rows_ref.shape[0] // peer_count
    step_count = capacity // GATHER_STEP

    def widen(turn, carry):
        lead = pl.multiple_of(turn * BLK, BLK)
        wide_ref[pl.ds(lead, BLK), :] = features_ref[pl.ds(lead, BLK), :].astype(WIDE)
        return carry

    lax.fori_loop(0, node_count // BLK, widen, 0, unroll=4)

    def one_peer(peer, carry):
        busy = (live_ref[peer] + GATHER_STEP - 1) // GATHER_STEP

        def fetch(step, inner):
            lead = pl.multiple_of(peer * capacity + step * GATHER_STEP, GATHER_STEP)
            for slot in range(GATHER_STEP):
                row = rows_ref[lead + slot]
                stage_ref[pl.ds(lead + slot, 1), :] = wide_ref[pl.ds(row, 1), :]
            return inner

        def blank(step, inner):
            lead = pl.multiple_of(peer * capacity + step * GATHER_STEP, GATHER_STEP)
            stage_ref[pl.ds(lead, GATHER_STEP), :] = jnp.zeros((GATHER_STEP, stage_ref.shape[1]), WIDE)
            return inner

        lax.fori_loop(0, busy, fetch, 0)
        lax.fori_loop(busy, step_count, blank, 0)
        return carry

    lax.fori_loop(0, peer_count, one_peer, 0)

    def narrow(turn, carry):
        lead = pl.multiple_of(turn * BLK, BLK)
        out_ref[pl.ds(lead, BLK), :] = stage_ref[pl.ds(lead, BLK), :].astype(LOW)
        return carry

    lax.fori_loop(0, peer_count * capacity // BLK, narrow, 0, unroll=4)


def spread(row):
    return jnp.broadcast_to(row, (SUB, BLK))


def leaky(values):
    return jnp.maximum(values, 0.2 * values)


def slope_of(values):
    return jnp.where(values > 0, 1.0, 0.2)


def at_block(index, blocks=1):
    return pl.ds(pl.multiple_of(index * blocks * BLK, BLK), blocks * BLK)


def column_sum(values):
    return jnp.sum(values, axis=0, keepdims=True)


def tile_steps():
    sub_index = lax.broadcasted_iota(jnp.int32, (SUB, BLK), 0)
    lane_index = lax.broadcasted_iota(jnp.int32, (SUB, BLK), 1)
    return (sub_index - lane_index) & (SUB - 1), lane_index


def tile_home():
    sub_index = lax.broadcasted_iota(jnp.int32, (SUB, BLK), 0)
    lane_index = lax.broadcasted_iota(jnp.int32, (SUB, BLK), 1)
    return (lane_index & (SUB - 1)) == sub_index


def skew(row):
    placed = jnp.where(tile_home(), spread(row), 0.0)
    placed = placed + pltpu.roll(placed, BLK - 1, 1)
    placed = placed + pltpu.roll(placed, BLK - 2, 1)
    return placed + pltpu.roll(placed, BLK - 4, 1)


def unskew(tile):
    tile = tile + pltpu.roll(tile, 1, 1)
    tile = tile + pltpu.roll(tile, 2, 1)
    tile = tile + pltpu.roll(tile, 4, 1)
    return column_sum(jnp.where(tile_home(), tile, 0.0))


def band_of(product):
    step_index, lane_index = tile_steps()
    tile_index = ((lane_index + step_index) & (BLK - 1)) // SUB
    band = product[:SUB]
    for part in range(1, BLK // SUB):
        band = jnp.where(tile_index == part, product[part * SUB : (part + 1) * SUB], band)
    return band


def project_into(rows, weight, weight_turned, proj_ref, projt_ref, index):
    proj_ref[index] = jnp.dot(rows, weight, preferred_element_type=WIDE).astype(LOW)
    turned = lax.dot_general(
        weight_turned, rows, (((1,), (1,)), ((), ())), preferred_element_type=WIDE
    ).astype(LOW)
    projt_ref[index] = turned
    return turned.astype(WIDE)


def own_kernel(
    local_pairs_ref,
    own_ref,
    weight_ref,
    consts_ref,
    cotangent_ref,
    projt_ref,
    score_ref,
    stats_ref,
    band_ref,
    bias_ref,
    proj_ref,
):
    block_count = own_ref.shape[0] // BLK
    local_count = local_pairs_ref.shape[1]
    weight = weight_ref[...]
    weight_turned = weight.astype(WIDE).T.astype(LOW)

    def one_table(block, grad_bias):
        nodes = at_block(block)
        turned = project_into(own_ref[nodes, :], weight, weight_turned, proj_ref, projt_ref, block)
        source = column_sum(turned * consts_ref[0])
        score_ref[block] = skew(source)
        upstream = cotangent_ref[:, nodes].astype(WIDE)
        stats_ref[block, 0:1, :] = source
        stats_ref[block, 1:2, :] = column_sum(turned * consts_ref[1])
        stats_ref[block, 2:3, :] = column_sum(upstream * turned)
        return grad_bias + upstream

    zero = jnp.zeros((weight.shape[1], BLK), WIDE)
    bias_ref[...] = lax.fori_loop(0, block_count, one_table, zero, unroll=8)

    def one_block(block, carry):
        upstream = cotangent_ref[:, at_block(block)]
        for pair in range(local_count):
            rows = proj_ref[local_pairs_ref[block, pair]]
            band_ref[block, pair] = band_of(jnp.dot(rows, upstream, preferred_element_type=WIDE))
        return carry

    lax.fori_loop(0, block_count, one_block, 0, unroll=2)


def layer_kernel(
    incoming_ref,
    local_pairs_ref,
    remote_pairs_ref,
    weight_ref,
    consts_ref,
    bias_ref,
    halo_hbm,
    own_projt_hbm,
    own_score_hbm,
    stats_hbm,
    cotangent_hbm,
    local_counts_hbm,
    remote_counts_hbm,
    band_hbm,
    own_hbm,
    out_hbm,
    shares_ref,
    halo_proj_ref,
    halo_projt_ref,
    halo_score_ref,
    own_grad_ref,
    halo_grad_ref,
    own_src_ref,
    halo_src_ref,
    own_rows_ref,
    mask_ref,
    halo_ref,
    own_projt_ref,
    own_score_ref,
    stats_ref,
    cotangent_ref,
    local_counts_ref,
    remote_counts_ref,
    band_ref,
    own_ref,
    out_ref,
    copy_sem,
):
    fetches = []
    for place, (source, target) in enumerate(
        (
            (halo_hbm, halo_ref),
            (own_projt_hbm, own_projt_ref),
            (own_score_hbm, own_score_ref),
            (stats_hbm, stats_ref),
            (cotangent_hbm, cotangent_ref),
            (local_counts_hbm, local_counts_ref),
            (remote_counts_hbm, remote_counts_ref),
            (band_hbm, band_ref),
            (own_hbm, own_ref),
        )
    ):
        fetches.append(pltpu.make_async_copy(source, target, copy_sem.at[place]))
    for fetch in fetches:
        fetch.start()
    block_count = own_ref.shape[0] // BLK
    halo_count = halo_ref.shape[0] // BLK
    local_count = local_pairs_ref.shape[1]
    remote_count = remote_pairs_ref.shape[1]
    pair_count = local_count + remote_count
    head_width = weight_ref.shape[1]
    step_index, lane_index = tile_steps()
    row_all = lax.broadcasted_iota(jnp.int32, (BLK, BLK), 0)
    lane_all = lax.broadcasted_iota(jnp.int32, (BLK, BLK), 1)
    mask_ref[...] = jnp.where(((row_all - lane_all) & (BLK - 1)) < SUB, 1.0, 0.0).astype(LOW)
    weight = weight_ref[...]
    weight_turned = weight.astype(WIDE).T.astype(LOW)

    own_grad_ref[...] = jnp.zeros(own_grad_ref.shape, WIDE)
    halo_grad_ref[...] = jnp.zeros(halo_grad_ref.shape, WIDE)
    own_src_ref[...] = jnp.zeros(own_src_ref.shape, WIDE)
    halo_src_ref[...] = jnp.zeros(halo_src_ref.shape, WIDE)

    fetches[0].wait()

    def halo_table(block, carry):
        rows = halo_ref[at_block(block), :]
        turned = project_into(
            rows, weight, weight_turned, halo_proj_ref, halo_projt_ref, block
        )
        source = column_sum(turned * consts_ref[0])
        slot = (block % PEER_BLOCKS) * BLK + lane_index[:1]
        live = slot < incoming_ref[block // PEER_BLOCKS]
        halo_score_ref[block] = skew(jnp.where(live, source, -jnp.inf))
        return carry

    lax.fori_loop(0, halo_count, halo_table, 0, unroll=16)

    def band_values(tiles):
        parts = []
        for tile in tiles:
            doubled = jnp.concatenate([tile, tile], 0).astype(LOW)
            for lead in range(0, BLK, 2 * SUB):
                parts.append(doubled * mask_ref[lead : lead + 2 * SUB, :])
        return jnp.concatenate(parts, 0)

    def one_block(block):
        nodes = at_block(block)
        upstream = cotangent_ref[:, nodes]
        upstream_wide = upstream.astype(WIDE)
        near = [local_pairs_ref[block, k] for k in range(local_count)]
        far = [remote_pairs_ref[block, k] for k in range(remote_count)]
        counts = [local_counts_ref[block, k : k + 1, :] for k in range(local_count)]
        counts += [remote_counts_ref[block, k : k + 1, :] for k in range(remote_count)]
        target_score = spread(stats_ref[block, 1:2, :])
        pre_self = target_score + spread(stats_ref[block, 0:1, :])
        logit_self = leaky(pre_self)
        pre = [target_score + own_score_ref[index] for index in near]
        pre += [target_score + halo_score_ref[index] for index in far]
        logits = [
            jnp.where(step_index < spread(count), leaky(value), -jnp.inf)
            for value, count in zip(pre, counts)
        ]
        top = logits[0]
        for logit in logits[1:]:
            top = jnp.maximum(top, logit)
        top = jnp.maximum(spread(jnp.max(top, axis=0, keepdims=True)), logit_self)
        raised = [jnp.exp(logit - top) for logit in logits]
        raised_self = jnp.exp(logit_self - top)
        denom = raised[0]
        for value in raised[1:]:
            denom = denom + value
        denom = spread(column_sum(denom)) + raised_self
        scale = 1.0 / denom
        share = [value * scale for value in raised]
        share_self = raised_self * scale
        sources = [own_projt_ref[index] for index in near]
        sources += [halo_projt_ref[index] for index in far]
        summed = None
        for lead in range(0, pair_count, WEIGHT_GROUP):
            group = slice(lead, lead + WEIGHT_GROUP)
            part = jnp.dot(
                jnp.concatenate(sources[group], 1),
                band_values(raised[group]),
                preferred_element_type=WIDE,
            )
            summed = part if summed is None else summed + part
        self_wide = own_projt_ref[block].astype(WIDE)
        aggregate = (summed + raised_self[:1] * self_wide) * scale[:1]
        out_ref[block] = (aggregate + consts_ref[2]).astype(LOW)
        inner = spread(column_sum(upstream_wide * aggregate))
        grad_self = share_self * (spread(stats_ref[block, 2:3, :]) - inner) * slope_of(pre_self)
        total = None
        for pair in range(pair_count):
            if pair < local_count:
                grad_share = band_ref[block, pair]
            else:
                rows = halo_proj_ref[far[pair - local_count]]
                grad_share = band_of(jnp.dot(rows, upstream, preferred_element_type=WIDE))
            grad_pre = share[pair] * (grad_share - inner) * slope_of(pre[pair])
            if pair < local_count:
                own_src_ref[near[pair]] += grad_pre
            else:
                halo_src_ref[far[pair - local_count]] += grad_pre
            total = grad_pre if total is None else total + grad_pre
        own_rows_ref[block, 0:1, :] = grad_self[:1]
        own_rows_ref[block, 1:2, :] = column_sum(total) + grad_self[:1]
        for lead in range(0, pair_count, SHARE_GROUP):
            grad_sources = lax.dot_general(
                upstream,
                band_values(share[lead : lead + SHARE_GROUP]),
                (((1,), (1,)), ((), ())),
                preferred_element_type=WIDE,
            )
            for pair in range(lead, min(lead + SHARE_GROUP, pair_count)):
                grad = grad_sources[:, (pair - lead) * BLK : (pair - lead + 1) * BLK]
                if pair < local_count:
                    own_grad_ref[near[pair]] += grad
                else:
                    halo_grad_ref[far[pair - local_count]] += grad
        own_grad_ref[block] += share_self[:1] * upstream_wide

    def one_turn(turn, carry):
        for part in range(TURN_BLOCKS):
            one_block(turn * TURN_BLOCKS + part)
        return carry

    for fetch in fetches[1:-1]:
        fetch.wait()
    lax.fori_loop(0, block_count // TURN_BLOCKS, one_turn, 0)
    store = pltpu.make_async_copy(out_ref, out_hbm, copy_sem.at[len(fetches)])
    store.start()
    fetches[-1].wait()

    def finish(index, rows, own, carry):
        grad_weight, from_src, from_dst = carry
        parts = []
        for part in range(2):
            at = index * 2 + part
            if own:
                turned = own_projt_ref[at].astype(WIDE)
                source = unskew(own_src_ref[at]) + own_rows_ref[at, 0:1, :]
                target = own_rows_ref[at, 1:2, :]
                grad = own_grad_ref[at] + consts_ref[0] * source + consts_ref[1] * target
                from_dst = from_dst + turned * target
            else:
                turned = halo_projt_ref[at].astype(WIDE)
                source = unskew(halo_src_ref[at])
                grad = halo_grad_ref[at] + consts_ref[0] * source
            from_src = from_src + turned * source
            high = grad.astype(LOW)
            low = (grad - high.astype(WIDE)).astype(LOW)
            parts.append(jnp.concatenate([high, low], 0))
        grad_weight = grad_weight + jnp.dot(
            jnp.concatenate(parts, 1), rows, preferred_element_type=WIDE
        )
        return grad_weight, from_src, from_dst

    def finish_own(index, carry):
        return finish(index, own_ref[at_block(index, 2), :], True, carry)

    def finish_halo(index, carry):
        return finish(index, halo_ref[at_block(index, 2), :], False, carry)

    zero = jnp.zeros((head_width, BLK), WIDE)
    carry = (jnp.zeros((2 * head_width, own_ref.shape[1]), WIDE), zero, zero)
    carry = lax.fori_loop(0, block_count // 2, finish_own, carry, unroll=8)
    carry = lax.fori_loop(0, halo_count // 2, finish_halo, carry, unroll=8)
    grad_weight, from_src, from_dst = carry
    grad_weight = grad_weight[:head_width] + grad_weight[head_width:]
    lanes = lax.broadcasted_iota(jnp.int32, (head_width, BLK), 1)
    extra = jnp.zeros((head_width, BLK), WIDE)
    for place, value in enumerate((from_src, from_dst, bias_ref[...])):
        extra = jnp.where(lanes == place, jnp.sum(value, axis=1, keepdims=True), extra)
    peers = shares_ref.shape[0]
    each = head_width // peers
    shares_ref[...] = jnp.zeros(shares_ref.shape, WIDE)
    for peer in range(peers):
        shares_ref[peer, :each, :] = grad_weight[peer * each : (peer + 1) * each]
        shares_ref[peer, each : 2 * each, :] = extra[peer * each : (peer + 1) * each]
    store.wait()


def relay_kernel(parts_ref, out_ref):
    total = parts_ref[0]
    for part in range(1, parts_ref.shape[0]):
        total = total + parts_ref[part]
    for copy in range(out_ref.shape[0]):
        out_ref[copy] = total


def keep_kernel(sums_ref, out_ref):
    out_ref[...] = sums_ref[0]


def last_kernel(me_ref, parts_ref, kept_ref, weight_ref, attention_ref, bias_ref, extra_ref):
    peers = parts_ref.shape[0]
    head_width = weight_ref.shape[0]
    each = head_width // peers
    extra_ref[...] = jnp.zeros(extra_ref.shape, WIDE)
    for peer in range(peers):
        weight_ref[peer * each : (peer + 1) * each, :] = parts_ref[peer, :each]
        extra_ref[peer * each : (peer + 1) * each, :] = parts_ref[peer, each : 2 * each]
    mine = pl.ds(me_ref[0] * each, each)
    weight_ref[mine, :] = kept_ref[:each]
    extra_ref[mine, :] = kept_ref[each : 2 * each]
    turned = extra_ref[...].T
    attention_ref[0] = turned[0:1, :head_width]
    attention_ref[1] = turned[1:2, :head_width]
    bias_ref[...] = turned[2:3, :head_width]


def vmem():
    return pl.BlockSpec(memory_space=pltpu.VMEM)


def anywhere():
    return pl.BlockSpec(memory_space=pl.ANY)


def smem():
    return pl.BlockSpec(memory_space=pltpu.SMEM)


def gather_rows(rows, live, features):
    slots = rows.shape[0]
    node_count, in_width = features.shape
    return pl.pallas_call(
        gather_kernel,
        out_shape=jax.ShapeDtypeStruct((slots, in_width), LOW),
        in_specs=[smem(), smem(), vmem()],
        out_specs=vmem(),
        scratch_shapes=[
            pltpu.VMEM((node_count, in_width), WIDE),
            pltpu.VMEM((slots, in_width), WIDE),
        ],
        compiler_params=pltpu.CompilerParams(vmem_limit_bytes=VMEM_LIMIT),
        name="gather_rows",
    )(rows, live, features)


def own_part(*operands):
    local_pairs, features, weight = operands[:3]
    head_width = weight.shape[1]
    block_count = features.shape[0] // BLK
    local_count = local_pairs.shape[1]
    tiles = jax.ShapeDtypeStruct((block_count, SUB, BLK), WIDE)
    return pl.pallas_call(
        own_kernel,
        out_shape=(
            jax.ShapeDtypeStruct((block_count, head_width, BLK), LOW),
            tiles,
            tiles,
            jax.ShapeDtypeStruct((block_count, local_count, SUB, BLK), WIDE),
            jax.ShapeDtypeStruct((head_width, BLK), WIDE),
        ),
        in_specs=[smem()] + [vmem()] * 4,
        out_specs=(vmem(),) * 5,
        scratch_shapes=[pltpu.VMEM((block_count, BLK, head_width), LOW)],
        compiler_params=pltpu.CompilerParams(vmem_limit_bytes=OWN_LIMIT),
        cost_estimate=pl.CostEstimate(flops=10**10, bytes_accessed=8 * 10**6, transcendentals=0),
        name="own_part",
    )(*operands)


def attention_layer(*operands):
    incoming, local_pairs, remote_pairs, weight = operands[:4]
    streamed = operands[6:]
    halo, cotangent = streamed[0], streamed[4]
    peer_count = incoming.shape[0]
    in_width = halo.shape[1]
    head_width, node_count = cotangent.shape
    block_count = node_count // BLK
    halo_count = halo.shape[0] // BLK
    return pl.pallas_call(
        layer_kernel,
        out_shape=(
            jax.ShapeDtypeStruct((block_count, head_width, BLK), LOW),
            jax.ShapeDtypeStruct((peer_count, SUB, in_width), WIDE),
        ),
        in_specs=[smem()] * 3 + [vmem()] * 3 + [anywhere()] * len(streamed),
        out_specs=(anywhere(), vmem()),
        scratch_shapes=[
            pltpu.VMEM((halo_count, BLK, head_width), LOW),
            pltpu.VMEM((halo_count, head_width, BLK), LOW),
            pltpu.VMEM((halo_count, SUB, BLK), WIDE),
            pltpu.VMEM((block_count, head_width, BLK), WIDE),
            pltpu.VMEM((halo_count, head_width, BLK), WIDE),
            pltpu.VMEM((block_count, SUB, BLK), WIDE),
            pltpu.VMEM((halo_count, SUB, BLK), WIDE),
            pltpu.VMEM((block_count, SUB, BLK), WIDE),
            pltpu.VMEM((BLK, BLK), LOW),
        ]
        + [pltpu.VMEM(value.shape, value.dtype) for value in streamed]
        + [
            pltpu.VMEM((block_count, head_width, BLK), LOW),
            pltpu.SemaphoreType.DMA((len(streamed) + 1,)),
        ],
        compiler_params=pltpu.CompilerParams(vmem_limit_bytes=LAYER_LIMIT),
        cost_estimate=pl.CostEstimate(flops=10**10, bytes_accessed=10**7, transcendentals=0),
        name="attention_layer",
    )(*operands)


def per_device(
    features,
    weight,
    attention,
    bias,
    cotangent,
    local_pairs,
    local_counts,
    remote_pairs,
    remote_counts,
    send_rows,
    send_counts,
):
    node_count, in_width = features.shape
    head_width = weight.shape[1]
    peer_count = lax.axis_size("dom")
    capacity = PEER_BLOCKS * BLK
    slots = peer_count * capacity
    me = lax.axis_index("dom")
    outgoing_live = lax.dynamic_index_in_dim(send_counts, me, 0, False)
    incoming_live = lax.dynamic_index_in_dim(send_counts, me, 1, False)
    outgoing = gather_rows(send_rows.reshape(-1), outgoing_live, features)
    halo = lax.all_to_all(
        outgoing.reshape(peer_count, capacity, in_width), "dom", 0, 0, tiled=True
    ).reshape(slots, in_width)
    consts = jnp.broadcast_to(
        jnp.concatenate([attention[:, 0], bias[None]], 0)[:, :, None], (3, head_width, BLK)
    )
    projt, score, stats, band, grad_bias = own_part(
        local_pairs, features, weight, consts, cotangent
    )
    output_blocks, shares = attention_layer(
        incoming_live,
        local_pairs,
        remote_pairs,
        weight,
        consts,
        grad_bias,
        halo,
        projt,
        score,
        stats,
        cotangent,
        local_counts,
        remote_counts,
        band,
        features,
    )
    output = output_blocks.transpose(1, 0, 2).reshape(head_width, node_count)
    partial_sums, output = lax.optimization_barrier((exchange(shares), output))
    chunk_sums = pl.pallas_call(
        relay_kernel,
        out_shape=jax.ShapeDtypeStruct(shares.shape, WIDE),
        in_specs=[vmem()],
        out_specs=vmem(),
        compiler_params=pltpu.CompilerParams(vmem_limit_bytes=SMALL_LIMIT),
        name="relay_sums",
    )(partial_sums)
    kept = pl.pallas_call(
        keep_kernel,
        out_shape=jax.ShapeDtypeStruct(shares.shape[1:], WIDE),
        in_specs=[vmem()],
        out_specs=vmem(),
        compiler_params=pltpu.CompilerParams(vmem_limit_bytes=SMALL_LIMIT),
        name="keep_own",
    )(chunk_sums)
    grad_weight, grad_attention, grad_bias = pl.pallas_call(
        last_kernel,
        out_shape=(
            jax.ShapeDtypeStruct((head_width, in_width), WIDE),
            jax.ShapeDtypeStruct((2, 1, head_width), WIDE),
            jax.ShapeDtypeStruct((1, head_width), WIDE),
        ),
        in_specs=[smem(), vmem(), vmem()],
        out_specs=(vmem(), vmem(), vmem()),
        scratch_shapes=[pltpu.VMEM((in_width, in_width), WIDE)],
        compiler_params=pltpu.CompilerParams(vmem_limit_bytes=SMALL_LIMIT),
        name="last_sums",
    )(me[None], exchange(chunk_sums), kept)
    return output, grad_weight.T, grad_attention, grad_bias[0]


def exchange(values):
    return lax.all_to_all(values, "dom", 0, 0, tiled=True)


def solution(mesh):
    return jax.shard_map(
        per_device,
        mesh=mesh,
        in_specs=(
            P("dom", None),
            P(None, "feat"),
            P(None, "feat", None),
            P("feat"),
            P("feat", "dom"),
            P("dom", None),
            P("dom", None, None),
            P("dom", None),
            P("dom", None, None),
            P("dom", None, None),
            P(),
        ),
        out_specs=(P("feat", "dom"), P(None, "feat"), P(None, "feat", None), P("feat")),
        check_vma=False,
    )
```

```python
import jax
import jax.numpy as jnp
from jax import lax
from jax.experimental import pallas as pl
from jax.experimental.pallas import tpu as pltpu
from jax.sharding import PartitionSpec as P

BLK = 128
PEER_BLOCKS = 2
SUB = 8
LOW = jnp.bfloat16
WIDE = jnp.float32
VMEM_LIMIT = 32 * 1024 * 1024
OWN_LIMIT = 62 * 1024 * 1024
SMALL_LIMIT = 4 * 1024 * 1024
LAYER_LIMIT = 60 * 1024 * 1024
TURN_BLOCKS = 16
WEIGHT_GROUP = 8
SHARE_GROUP = 2
GATHER_STEP = 32


def gather_kernel(rows_ref, live_ref, features_ref, out_ref, wide_ref, stage_ref):
    node_count = features_ref.shape[0]
    peer_count = live_ref.shape[0]
    capacity = rows_ref.shape[0] // peer_count
    step_count = capacity // GATHER_STEP

    def widen(turn, carry):
        lead = pl.multiple_of(turn * BLK, BLK)
        wide_ref[pl.ds(lead, BLK), :] = features_ref[pl.ds(lead, BLK), :].astype(WIDE)
        return carry

    lax.fori_loop(0, node_count // BLK, widen, 0, unroll=4)

    def one_peer(peer, carry):
        busy = (live_ref[peer] + GATHER_STEP - 1) // GATHER_STEP

        def fetch(step, inner):
            lead = pl.multiple_of(peer * capacity + step * GATHER_STEP, GATHER_STEP)
            for slot in range(GATHER_STEP):
                row = rows_ref[lead + slot]
                stage_ref[pl.ds(lead + slot, 1), :] = wide_ref[pl.ds(row, 1), :]
            return inner

        def blank(step, inner):
            lead = pl.multiple_of(peer * capacity + step * GATHER_STEP, GATHER_STEP)
            stage_ref[pl.ds(lead, GATHER_STEP), :] = jnp.zeros((GATHER_STEP, stage_ref.shape[1]), WIDE)
            return inner

        lax.fori_loop(0, busy, fetch, 0)
        lax.fori_loop(busy, step_count, blank, 0)
        return carry

    lax.fori_loop(0, peer_count, one_peer, 0)

    def narrow(turn, carry):
        lead = pl.multiple_of(turn * BLK, BLK)
        out_ref[pl.ds(lead, BLK), :] = stage_ref[pl.ds(lead, BLK), :].astype(LOW)
        return carry

    lax.fori_loop(0, peer_count * capacity // BLK, narrow, 0, unroll=4)


def spread(row):
    return jnp.broadcast_to(row, (SUB, BLK))


def leaky(values):
    return jnp.maximum(values, 0.2 * values)


def slope_of(values):
    return jnp.where(values > 0, 1.0, 0.2)


def at_block(index, blocks=1):
    return pl.ds(pl.multiple_of(index * blocks * BLK, BLK), blocks * BLK)


def column_sum(values):
    return jnp.sum(values, axis=0, keepdims=True)


def tile_steps():
    sub_index = lax.broadcasted_iota(jnp.int32, (SUB, BLK), 0)
    lane_index = lax.broadcasted_iota(jnp.int32, (SUB, BLK), 1)
    return (sub_index - lane_index) & (SUB - 1), lane_index


def tile_home():
    sub_index = lax.broadcasted_iota(jnp.int32, (SUB, BLK), 0)
    lane_index = lax.broadcasted_iota(jnp.int32, (SUB, BLK), 1)
    return (lane_index & (SUB - 1)) == sub_index


def skew(row):
    placed = jnp.where(tile_home(), spread(row), 0.0)
    placed = placed + pltpu.roll(placed, BLK - 1, 1)
    placed = placed + pltpu.roll(placed, BLK - 2, 1)
    return placed + pltpu.roll(placed, BLK - 4, 1)


def unskew(tile):
    tile = tile + pltpu.roll(tile, 1, 1)
    tile = tile + pltpu.roll(tile, 2, 1)
    tile = tile + pltpu.roll(tile, 4, 1)
    return column_sum(jnp.where(tile_home(), tile, 0.0))


def band_of(product):
    step_index, lane_index = tile_steps()
    tile_index = ((lane_index + step_index) & (BLK - 1)) // SUB
    band = product[:SUB]
    for part in range(1, BLK // SUB):
        band = jnp.where(tile_index == part, product[part * SUB : (part + 1) * SUB], band)
    return band


def project_into(rows, weight, weight_turned, proj_ref, projt_ref, index):
    proj_ref[index] = jnp.dot(rows, weight, preferred_element_type=WIDE).astype(LOW)
    turned = lax.dot_general(
        weight_turned, rows, (((1,), (1,)), ((), ())), preferred_element_type=WIDE
    ).astype(LOW)
    projt_ref[index] = turned
    return turned.astype(WIDE)


def own_kernel(
    pairs_ref,
    own_ref,
    weight_ref,
    consts_ref,
    cotangent_ref,
    projt_ref,
    score_ref,
    stats_ref,
    band_ref,
    bias_ref,
    proj_ref,
):
    block_count = own_ref.shape[0] // BLK
    local_count = band_ref.shape[1]
    pair_count = pairs_ref.shape[0] // block_count
    weight = weight_ref[...]
    weight_turned = weight.astype(WIDE).T.astype(LOW)

    def one_table(block, grad_bias):
        nodes = at_block(block)
        turned = project_into(own_ref[nodes, :], weight, weight_turned, proj_ref, projt_ref, block)
        source = column_sum(turned * consts_ref[0])
        score_ref[block] = skew(source)
        upstream = cotangent_ref[:, nodes].astype(WIDE)
        stats_ref[block, 0:1, :] = source
        stats_ref[block, 1:2, :] = column_sum(turned * consts_ref[1])
        stats_ref[block, 2:3, :] = column_sum(upstream * turned)
        return grad_bias + upstream

    zero = jnp.zeros((weight.shape[1], BLK), WIDE)
    bias_ref[...] = lax.fori_loop(0, block_count, one_table, zero, unroll=8)

    def one_block(block, carry):
        upstream = cotangent_ref[:, at_block(block)]
        for pair in range(local_count):
            rows = proj_ref[pairs_ref[block * pair_count + pair]]
            band_ref[block, pair] = band_of(jnp.dot(rows, upstream, preferred_element_type=WIDE))
        return carry

    lax.fori_loop(0, block_count, one_block, 0, unroll=2)


def layer_kernel(
    incoming_ref,
    pairs_ref,
    weight_ref,
    consts_ref,
    bias_ref,
    halo_hbm,
    own_projt_hbm,
    own_score_hbm,
    stats_hbm,
    cotangent_hbm,
    local_counts_hbm,
    remote_counts_hbm,
    band_hbm,
    own_hbm,
    out_hbm,
    shares_ref,
    halo_proj_ref,
    halo_projt_ref,
    halo_score_ref,
    own_grad_ref,
    halo_grad_ref,
    own_src_ref,
    halo_src_ref,
    own_rows_ref,
    mask_ref,
    halo_ref,
    own_projt_ref,
    own_score_ref,
    stats_ref,
    cotangent_ref,
    local_counts_ref,
    remote_counts_ref,
    band_ref,
    own_ref,
    out_ref,
    copy_sem,
):
    fetches = []
    for place, (source, target) in enumerate(
        (
            (halo_hbm, halo_ref),
            (own_projt_hbm, own_projt_ref),
            (own_score_hbm, own_score_ref),
            (stats_hbm, stats_ref),
            (cotangent_hbm, cotangent_ref),
            (local_counts_hbm, local_counts_ref),
            (remote_counts_hbm, remote_counts_ref),
            (band_hbm, band_ref),
            (own_hbm, own_ref),
        )
    ):
        fetches.append(pltpu.make_async_copy(source, target, copy_sem.at[place]))
    for fetch in fetches:
        fetch.start()
    block_count = own_ref.shape[0] // BLK
    halo_count = halo_ref.shape[0] // BLK
    local_count = band_ref.shape[1]
    pair_count = pairs_ref.shape[0] // block_count
    remote_count = pair_count - local_count
    head_width = weight_ref.shape[1]
    step_index, lane_index = tile_steps()
    row_all = lax.broadcasted_iota(jnp.int32, (BLK, BLK), 0)
    lane_all = lax.broadcasted_iota(jnp.int32, (BLK, BLK), 1)
    mask_ref[...] = jnp.where(((row_all - lane_all) & (BLK - 1)) < SUB, 1.0, 0.0).astype(LOW)
    weight = weight_ref[...]
    weight_turned = weight.astype(WIDE).T.astype(LOW)

    own_grad_ref[...] = jnp.zeros(own_grad_ref.shape, WIDE)
    halo_grad_ref[...] = jnp.zeros(halo_grad_ref.shape, WIDE)
    own_src_ref[...] = jnp.zeros(own_src_ref.shape, WIDE)
    halo_src_ref[...] = jnp.zeros(halo_src_ref.shape, WIDE)

    fetches[0].wait()

    def halo_table(block, carry):
        rows = halo_ref[at_block(block), :]
        turned = project_into(
            rows, weight, weight_turned, halo_proj_ref, halo_projt_ref, block
        )
        source = column_sum(turned * consts_ref[0])
        slot = (block % PEER_BLOCKS) * BLK + lane_index[:1]
        live = slot < incoming_ref[block // PEER_BLOCKS]
        halo_score_ref[block] = skew(jnp.where(live, source, -jnp.inf))
        return carry

    lax.fori_loop(0, halo_count, halo_table, 0, unroll=32)

    def band_values(tiles):
        parts = []
        for tile in tiles:
            doubled = jnp.concatenate([tile, tile], 0).astype(LOW)
            for lead in range(0, BLK, 2 * SUB):
                parts.append(doubled * mask_ref[lead : lead + 2 * SUB, :])
        return jnp.concatenate(parts, 0)

    def one_block(block):
        nodes = at_block(block)
        upstream = cotangent_ref[:, nodes]
        upstream_wide = upstream.astype(WIDE)
        near = [pairs_ref[block * pair_count + k] for k in range(local_count)]
        far = [pairs_ref[block * pair_count + k] for k in range(local_count, pair_count)]
        counts = [local_counts_ref[block, k : k + 1, :] for k in range(local_count)]
        counts += [remote_counts_ref[block, k : k + 1, :] for k in range(remote_count)]
        target_score = spread(stats_ref[block, 1:2, :])
        pre_self = target_score + spread(stats_ref[block, 0:1, :])
        logit_self = leaky(pre_self)
        pre = [target_score + own_score_ref[index] for index in near]
        pre += [target_score + halo_score_ref[index] for index in far]
        logits = [
            jnp.where(step_index < spread(count), leaky(value), -jnp.inf)
            for value, count in zip(pre, counts)
        ]
        top = logits[0]
        for logit in logits[1:]:
            top = jnp.maximum(top, logit)
        top = jnp.maximum(spread(jnp.max(top, axis=0, keepdims=True)), logit_self)
        raised = [jnp.exp(logit - top) for logit in logits]
        raised_self = jnp.exp(logit_self - top)
        denom = raised[0]
        for value in raised[1:]:
            denom = denom + value
        denom = spread(column_sum(denom)) + raised_self
        scale = 1.0 / denom
        share = [value * scale for value in raised]
        share_self = raised_self * scale
        sources = [own_projt_ref[index] for index in near]
        sources += [halo_projt_ref[index] for index in far]
        summed = None
        for lead in range(0, pair_count, WEIGHT_GROUP):
            group = slice(lead, lead + WEIGHT_GROUP)
            part = jnp.dot(
                jnp.concatenate(sources[group], 1),
                band_values(raised[group]),
                preferred_element_type=WIDE,
            )
            summed = part if summed is None else summed + part
        self_wide = own_projt_ref[block].astype(WIDE)
        aggregate = (summed + raised_self[:1] * self_wide) * scale[:1]
        out_ref[block] = (aggregate + consts_ref[2]).astype(LOW)
        inner = spread(column_sum(upstream_wide * aggregate))
        grad_self = share_self * (spread(stats_ref[block, 2:3, :]) - inner) * slope_of(pre_self)
        total = None
        for pair in range(pair_count):
            if pair < local_count:
                grad_share = band_ref[block, pair]
            else:
                rows = halo_proj_ref[far[pair - local_count]]
                grad_share = band_of(jnp.dot(rows, upstream, preferred_element_type=WIDE))
            grad_pre = share[pair] * (grad_share - inner) * slope_of(pre[pair])
            if pair < local_count:
                own_src_ref[near[pair]] += grad_pre
            else:
                halo_src_ref[far[pair - local_count]] += grad_pre
            total = grad_pre if total is None else total + grad_pre
        own_rows_ref[block, 0:1, :] = grad_self[:1]
        own_rows_ref[block, 1:2, :] = column_sum(total) + grad_self[:1]
        for lead in range(0, pair_count, SHARE_GROUP):
            grad_sources = lax.dot_general(
                upstream,
                band_values(share[lead : lead + SHARE_GROUP]),
                (((1,), (1,)), ((), ())),
                preferred_element_type=WIDE,
            )
            for pair in range(lead, min(lead + SHARE_GROUP, pair_count)):
                grad = grad_sources[:, (pair - lead) * BLK : (pair - lead + 1) * BLK]
                if pair < local_count:
                    own_grad_ref[near[pair]] += grad
                else:
                    halo_grad_ref[far[pair - local_count]] += grad
        own_grad_ref[block] += share_self[:1] * upstream_wide

    def one_turn(turn, carry):
        for part in range(TURN_BLOCKS):
            one_block(turn * TURN_BLOCKS + part)
        return carry

    for fetch in fetches[1:-1]:
        fetch.wait()
    lax.fori_loop(0, block_count // TURN_BLOCKS, one_turn, 0)
    store = pltpu.make_async_copy(out_ref, out_hbm, copy_sem.at[len(fetches)])
    store.start()
    fetches[-1].wait()

    def finish(index, rows, own, carry):
        grad_weight, from_src, from_dst = carry
        parts = []
        for part in range(8):
            at = index * 8 + part
            if own:
                turned = own_projt_ref[at].astype(WIDE)
                source = unskew(own_src_ref[at]) + own_rows_ref[at, 0:1, :]
                target = own_rows_ref[at, 1:2, :]
                grad = own_grad_ref[at] + consts_ref[0] * source + consts_ref[1] * target
                from_dst = from_dst + turned * target
            else:
                turned = halo_projt_ref[at].astype(WIDE)
                source = unskew(halo_src_ref[at])
                grad = halo_grad_ref[at] + consts_ref[0] * source
            from_src = from_src + turned * source
            high = grad.astype(LOW)
            low = (grad - high.astype(WIDE)).astype(LOW)
            parts.append(jnp.concatenate([high, low], 0))
        grad_weight = grad_weight + jnp.dot(
            jnp.concatenate(parts, 1), rows, preferred_element_type=WIDE
        )
        return grad_weight, from_src, from_dst

    def finish_own(index, carry):
        return finish(index, own_ref[at_block(index, 8), :], True, carry)

    def finish_halo(index, carry):
        return finish(index, halo_ref[at_block(index, 8), :], False, carry)

    zero = jnp.zeros((head_width, BLK), WIDE)
    carry = (jnp.zeros((2 * head_width, own_ref.shape[1]), WIDE), zero, zero)
    carry = lax.fori_loop(0, block_count // 8, finish_own, carry, unroll=8)
    carry = lax.fori_loop(0, halo_count // 8, finish_halo, carry, unroll=8)
    grad_weight, from_src, from_dst = carry
    grad_weight = grad_weight[:head_width] + grad_weight[head_width:]
    lanes = lax.broadcasted_iota(jnp.int32, (head_width, BLK), 1)
    extra = jnp.zeros((head_width, BLK), WIDE)
    for place, value in enumerate((from_src, from_dst, bias_ref[...])):
        extra = jnp.where(lanes == place, jnp.sum(value, axis=1, keepdims=True), extra)
    peers = shares_ref.shape[0]
    each = head_width // peers
    shares_ref[...] = jnp.zeros(shares_ref.shape, WIDE)
    for peer in range(peers):
        shares_ref[peer, :each, :] = grad_weight[peer * each : (peer + 1) * each]
        shares_ref[peer, each : 2 * each, :] = extra[peer * each : (peer + 1) * each]
    store.wait()


def relay_kernel(parts_ref, out_ref):
    total = parts_ref[0]
    for part in range(1, parts_ref.shape[0]):
        total = total + parts_ref[part]
    for copy in range(out_ref.shape[0]):
        out_ref[copy] = total


def keep_kernel(sums_ref, out_ref):
    out_ref[...] = sums_ref[0]


def last_kernel(me_ref, parts_ref, kept_ref, weight_ref, attention_ref, bias_ref, extra_ref):
    peers = parts_ref.shape[0]
    head_width = weight_ref.shape[0]
    each = head_width // peers
    extra_ref[...] = jnp.zeros(extra_ref.shape, WIDE)
    for peer in range(peers):
        weight_ref[peer * each : (peer + 1) * each, :] = parts_ref[peer, :each]
        extra_ref[peer * each : (peer + 1) * each, :] = parts_ref[peer, each : 2 * each]
    mine = pl.ds(me_ref[0] * each, each)
    weight_ref[mine, :] = kept_ref[:each]
    extra_ref[mine, :] = kept_ref[each : 2 * each]
    turned = extra_ref[...].T
    attention_ref[0] = turned[0:1, :head_width]
    attention_ref[1] = turned[1:2, :head_width]
    bias_ref[...] = turned[2:3, :head_width]


def vmem():
    return pl.BlockSpec(memory_space=pltpu.VMEM)


def anywhere():
    return pl.BlockSpec(memory_space=pl.ANY)


def smem():
    return pl.BlockSpec(memory_space=pltpu.SMEM)


def gather_rows(rows, live, features):
    slots = rows.shape[0]
    node_count, in_width = features.shape
    return pl.pallas_call(
        gather_kernel,
        out_shape=jax.ShapeDtypeStruct((slots, in_width), LOW),
        in_specs=[smem(), smem(), vmem()],
        out_specs=vmem(),
        scratch_shapes=[
            pltpu.VMEM((node_count, in_width), WIDE),
            pltpu.VMEM((slots, in_width), WIDE),
        ],
        compiler_params=pltpu.CompilerParams(vmem_limit_bytes=VMEM_LIMIT),
        name="gather_rows",
    )(rows, live, features)


def own_part(local_count, *operands):
    pairs, features, weight = operands[:3]
    head_width = weight.shape[1]
    block_count = features.shape[0] // BLK
    tiles = jax.ShapeDtypeStruct((block_count, SUB, BLK), WIDE)
    return pl.pallas_call(
        own_kernel,
        out_shape=(
            jax.ShapeDtypeStruct((block_count, head_width, BLK), LOW),
            tiles,
            tiles,
            jax.ShapeDtypeStruct((block_count, local_count, SUB, BLK), WIDE),
            jax.ShapeDtypeStruct((head_width, BLK), WIDE),
        ),
        in_specs=[smem()] + [vmem()] * 4,
        out_specs=(vmem(),) * 5,
        scratch_shapes=[pltpu.VMEM((block_count, BLK, head_width), LOW)],
        compiler_params=pltpu.CompilerParams(vmem_limit_bytes=OWN_LIMIT),
        cost_estimate=pl.CostEstimate(flops=10**10, bytes_accessed=8 * 10**6, transcendentals=0),
        name="own_part",
    )(*operands)


def attention_layer(*operands):
    incoming, pairs, weight = operands[:3]
    streamed = operands[5:]
    halo, cotangent = streamed[0], streamed[4]
    peer_count = incoming.shape[0]
    in_width = halo.shape[1]
    head_width, node_count = cotangent.shape
    block_count = node_count // BLK
    halo_count = halo.shape[0] // BLK
    return pl.pallas_call(
        layer_kernel,
        out_shape=(
            jax.ShapeDtypeStruct((block_count, head_width, BLK), LOW),
            jax.ShapeDtypeStruct((peer_count, SUB, in_width), WIDE),
        ),
        in_specs=[smem()] * 2 + [vmem()] * 3 + [anywhere()] * len(streamed),
        out_specs=(anywhere(), vmem()),
        scratch_shapes=[
            pltpu.VMEM((halo_count, BLK, head_width), LOW),
            pltpu.VMEM((halo_count, head_width, BLK), LOW),
            pltpu.VMEM((halo_count, SUB, BLK), WIDE),
            pltpu.VMEM((block_count, head_width, BLK), WIDE),
            pltpu.VMEM((halo_count, head_width, BLK), WIDE),
            pltpu.VMEM((block_count, SUB, BLK), WIDE),
            pltpu.VMEM((halo_count, SUB, BLK), WIDE),
            pltpu.VMEM((block_count, SUB, BLK), WIDE),
            pltpu.VMEM((BLK, BLK), LOW),
        ]
        + [pltpu.VMEM(value.shape, value.dtype) for value in streamed]
        + [
            pltpu.VMEM((block_count, head_width, BLK), LOW),
            pltpu.SemaphoreType.DMA((len(streamed) + 1,)),
        ],
        compiler_params=pltpu.CompilerParams(vmem_limit_bytes=LAYER_LIMIT),
        cost_estimate=pl.CostEstimate(flops=10**10, bytes_accessed=10**7, transcendentals=0),
        name="attention_layer",
    )(*operands)


def per_device(
    features,
    weight,
    attention,
    bias,
    cotangent,
    local_pairs,
    local_counts,
    remote_pairs,
    remote_counts,
    send_rows,
    send_counts,
):
    node_count, in_width = features.shape
    head_width = weight.shape[1]
    peer_count = lax.axis_size("dom")
    capacity = PEER_BLOCKS * BLK
    slots = peer_count * capacity
    me = lax.axis_index("dom")
    outgoing_live = lax.dynamic_index_in_dim(send_counts, me, 0, False)
    incoming_live = lax.dynamic_index_in_dim(send_counts, me, 1, False)
    outgoing = gather_rows(send_rows.reshape(-1), outgoing_live, features)
    halo = lax.all_to_all(
        outgoing.reshape(peer_count, capacity, in_width), "dom", 0, 0, tiled=True
    ).reshape(slots, in_width)
    consts = jnp.broadcast_to(
        jnp.concatenate([attention[:, 0], bias[None]], 0)[:, :, None], (3, head_width, BLK)
    )
    pairs = jnp.concatenate([local_pairs, remote_pairs], 1).reshape(-1)
    projt, score, stats, band, grad_bias = own_part(
        local_pairs.shape[1], pairs, features, weight, consts, cotangent
    )
    output_blocks, shares = attention_layer(
        incoming_live,
        pairs,
        weight,
        consts,
        grad_bias,
        halo,
        projt,
        score,
        stats,
        cotangent,
        local_counts,
        remote_counts,
        band,
        features,
    )
    output = output_blocks.transpose(1, 0, 2).reshape(head_width, node_count)
    partial_sums, output = lax.optimization_barrier((exchange(shares), output))
    chunk_sums = pl.pallas_call(
        relay_kernel,
        out_shape=jax.ShapeDtypeStruct(shares.shape, WIDE),
        in_specs=[vmem()],
        out_specs=vmem(),
        compiler_params=pltpu.CompilerParams(vmem_limit_bytes=SMALL_LIMIT),
        name="relay_sums",
    )(partial_sums)
    kept = pl.pallas_call(
        keep_kernel,
        out_shape=jax.ShapeDtypeStruct(shares.shape[1:], WIDE),
        in_specs=[vmem()],
        out_specs=vmem(),
        compiler_params=pltpu.CompilerParams(vmem_limit_bytes=SMALL_LIMIT),
        name="keep_own",
    )(chunk_sums)
    grad_weight, grad_attention, grad_bias = pl.pallas_call(
        last_kernel,
        out_shape=(
            jax.ShapeDtypeStruct((head_width, in_width), WIDE),
            jax.ShapeDtypeStruct((2, 1, head_width), WIDE),
            jax.ShapeDtypeStruct((1, head_width), WIDE),
        ),
        in_specs=[smem(), vmem(), vmem()],
        out_specs=(vmem(), vmem(), vmem()),
        scratch_shapes=[pltpu.VMEM((in_width, in_width), WIDE)],
        compiler_params=pltpu.CompilerParams(vmem_limit_bytes=SMALL_LIMIT),
        name="last_sums",
    )(me[None], exchange(chunk_sums), kept)
    return output, grad_weight.T, grad_attention, grad_bias[0]


def exchange(values):
    return lax.all_to_all(values, "dom", 0, 0, tiled=True)


def solution(mesh):
    return jax.shard_map(
        per_device,
        mesh=mesh,
        in_specs=(
            P("dom", None),
            P(None, "feat"),
            P(None, "feat", None),
            P("feat"),
            P("feat", "dom"),
            P("dom", None),
            P("dom", None, None),
            P("dom", None),
            P("dom", None, None),
            P("dom", None, None),
            P(),
        ),
        out_specs=(P("feat", "dom"), P(None, "feat"), P(None, "feat", None), P("feat")),
        check_vma=False,
    )
```

```python
import jax
import jax.numpy as jnp
from jax import lax
from jax.experimental import pallas as pl
from jax.experimental.pallas import tpu as pltpu
from jax.sharding import PartitionSpec as P

BLK = 128
PEER_BLOCKS = 2
SUB = 8
LOW = jnp.bfloat16
WIDE = jnp.float32
VMEM_LIMIT = 32 * 1024 * 1024
OWN_LIMIT = 62 * 1024 * 1024
SMALL_LIMIT = 4 * 1024 * 1024
LAYER_LIMIT = 60 * 1024 * 1024
TURN_BLOCKS = 16
NEAR_GROUP = 4
WEIGHT_GROUP = 8
SHARE_GROUP = 2
GATHER_STEP = 32


def gather_kernel(rows_ref, live_ref, features_ref, out_ref, wide_ref, stage_ref):
    node_count = features_ref.shape[0]
    peer_count = live_ref.shape[0]
    capacity = rows_ref.shape[0] // peer_count
    step_count = capacity // GATHER_STEP

    def widen(turn, carry):
        lead = pl.multiple_of(turn * BLK, BLK)
        wide_ref[pl.ds(lead, BLK), :] = features_ref[pl.ds(lead, BLK), :].astype(WIDE)
        return carry

    lax.fori_loop(0, node_count // BLK, widen, 0, unroll=4)

    def one_peer(peer, carry):
        busy = (live_ref[peer] + GATHER_STEP - 1) // GATHER_STEP

        def fetch(step, inner):
            lead = pl.multiple_of(peer * capacity + step * GATHER_STEP, GATHER_STEP)
            for slot in range(GATHER_STEP):
                row = rows_ref[lead + slot]
                stage_ref[pl.ds(lead + slot, 1), :] = wide_ref[pl.ds(row, 1), :]
            return inner

        def blank(step, inner):
            lead = pl.multiple_of(peer * capacity + step * GATHER_STEP, GATHER_STEP)
            stage_ref[pl.ds(lead, GATHER_STEP), :] = jnp.zeros((GATHER_STEP, stage_ref.shape[1]), WIDE)
            return inner

        lax.fori_loop(0, busy, fetch, 0)
        lax.fori_loop(busy, step_count, blank, 0)
        return carry

    lax.fori_loop(0, peer_count, one_peer, 0)

    def narrow(turn, carry):
        lead = pl.multiple_of(turn * BLK, BLK)
        out_ref[pl.ds(lead, BLK), :] = stage_ref[pl.ds(lead, BLK), :].astype(LOW)
        return carry

    lax.fori_loop(0, peer_count * capacity // BLK, narrow, 0, unroll=4)


def spread(row):
    return jnp.broadcast_to(row, (SUB, BLK))


def leaky(values):
    return jnp.maximum(values, 0.2 * values)


def slope_of(values):
    return jnp.where(values > 0, 1.0, 0.2)


def at_block(index, blocks=1):
    return pl.ds(pl.multiple_of(index * blocks * BLK, BLK), blocks * BLK)


def column_sum(values):
    return jnp.sum(values, axis=0, keepdims=True)


def tile_steps():
    sub_index = lax.broadcasted_iota(jnp.int32, (SUB, BLK), 0)
    lane_index = lax.broadcasted_iota(jnp.int32, (SUB, BLK), 1)
    return (sub_index - lane_index) & (SUB - 1), lane_index


def tile_home():
    sub_index = lax.broadcasted_iota(jnp.int32, (SUB, BLK), 0)
    lane_index = lax.broadcasted_iota(jnp.int32, (SUB, BLK), 1)
    return (lane_index & (SUB - 1)) == sub_index


def skew(row):
    placed = jnp.where(tile_home(), spread(row), 0.0)
    placed = placed + pltpu.roll(placed, BLK - 1, 1)
    placed = placed + pltpu.roll(placed, BLK - 2, 1)
    return placed + pltpu.roll(placed, BLK - 4, 1)


def unskew(tile):
    tile = tile + pltpu.roll(tile, 1, 1)
    tile = tile + pltpu.roll(tile, 2, 1)
    tile = tile + pltpu.roll(tile, 4, 1)
    return column_sum(jnp.where(tile_home(), tile, 0.0))


def band_of(product):
    step_index, lane_index = tile_steps()
    tile_index = ((lane_index + step_index) & (BLK - 1)) // SUB
    band = product[:SUB]
    for part in range(1, BLK // SUB):
        band = jnp.where(tile_index == part, product[part * SUB : (part + 1) * SUB], band)
    return band


def project_into(rows, weight, weight_turned, proj_ref, projt_ref, index):
    proj_ref[index] = jnp.dot(rows, weight, preferred_element_type=WIDE).astype(LOW)
    turned = lax.dot_general(
        weight_turned, rows, (((1,), (1,)), ((), ())), preferred_element_type=WIDE
    ).astype(LOW)
    projt_ref[index] = turned
    return turned.astype(WIDE)


def own_kernel(
    pairs_ref,
    own_ref,
    weight_ref,
    consts_ref,
    cotangent_ref,
    projt_ref,
    score_ref,
    stats_ref,
    band_ref,
    bias_ref,
    proj_ref,
):
    block_count = own_ref.shape[0] // BLK
    local_count = band_ref.shape[1]
    pair_count = pairs_ref.shape[0] // block_count
    weight = weight_ref[...]
    weight_turned = weight.astype(WIDE).T.astype(LOW)

    def one_table(block, grad_bias):
        nodes = at_block(block)
        turned = project_into(own_ref[nodes, :], weight, weight_turned, proj_ref, projt_ref, block)
        source = column_sum(turned * consts_ref[0])
        score_ref[block] = skew(source)
        upstream = cotangent_ref[:, nodes].astype(WIDE)
        stats_ref[block, 0:1, :] = source
        stats_ref[block, 1:2, :] = column_sum(turned * consts_ref[1])
        stats_ref[block, 2:3, :] = column_sum(upstream * turned)
        return grad_bias + upstream

    zero = jnp.zeros((weight.shape[1], BLK), WIDE)
    bias_ref[...] = lax.fori_loop(0, block_count, one_table, zero, unroll=8)

    def one_block(block, carry):
        upstream = cotangent_ref[:, at_block(block)]
        for pair in range(local_count):
            rows = proj_ref[pairs_ref[block * pair_count + pair]]
            band_ref[block, pair] = band_of(jnp.dot(rows, upstream, preferred_element_type=WIDE))
        return carry

    lax.fori_loop(0, block_count, one_block, 0, unroll=2)


def layer_kernel(
    incoming_ref,
    pairs_ref,
    weight_ref,
    consts_ref,
    bias_ref,
    halo_hbm,
    own_projt_hbm,
    own_score_hbm,
    stats_hbm,
    cotangent_hbm,
    local_counts_hbm,
    remote_counts_hbm,
    band_hbm,
    own_hbm,
    out_hbm,
    shares_ref,
    halo_proj_ref,
    halo_projt_ref,
    halo_score_ref,
    own_grad_ref,
    halo_grad_ref,
    own_src_ref,
    halo_src_ref,
    own_rows_ref,
    mask_ref,
    halo_ref,
    own_projt_ref,
    own_score_ref,
    stats_ref,
    cotangent_ref,
    local_counts_ref,
    remote_counts_ref,
    band_ref,
    own_ref,
    out_ref,
    copy_sem,
):
    fetches = []
    for place, (source, target) in enumerate(
        (
            (halo_hbm, halo_ref),
            (own_projt_hbm, own_projt_ref),
            (own_score_hbm, own_score_ref),
            (stats_hbm, stats_ref),
            (cotangent_hbm, cotangent_ref),
            (local_counts_hbm, local_counts_ref),
            (remote_counts_hbm, remote_counts_ref),
            (band_hbm, band_ref),
            (own_hbm, own_ref),
        )
    ):
        fetches.append(pltpu.make_async_copy(source, target, copy_sem.at[place]))
    for fetch in fetches:
        fetch.start()
    block_count = own_ref.shape[0] // BLK
    halo_count = halo_ref.shape[0] // BLK
    local_count = band_ref.shape[1]
    pair_count = pairs_ref.shape[0] // block_count
    remote_count = pair_count - local_count
    head_width = weight_ref.shape[1]
    step_index, lane_index = tile_steps()
    row_all = lax.broadcasted_iota(jnp.int32, (BLK, BLK), 0)
    lane_all = lax.broadcasted_iota(jnp.int32, (BLK, BLK), 1)
    mask_ref[...] = jnp.where(((row_all - lane_all) & (BLK - 1)) < SUB, 1.0, 0.0).astype(LOW)
    weight = weight_ref[...]
    weight_turned = weight.astype(WIDE).T.astype(LOW)

    own_grad_ref[...] = jnp.zeros(own_grad_ref.shape, WIDE)
    halo_grad_ref[...] = jnp.zeros(halo_grad_ref.shape, WIDE)
    own_src_ref[...] = jnp.zeros(own_src_ref.shape, WIDE)
    halo_src_ref[...] = jnp.zeros(halo_src_ref.shape, WIDE)

    fetches[0].wait()

    def halo_table(block, carry):
        rows = halo_ref[at_block(block), :]
        turned = project_into(
            rows, weight, weight_turned, halo_proj_ref, halo_projt_ref, block
        )
        source = column_sum(turned * consts_ref[0])
        slot = (block % PEER_BLOCKS) * BLK + lane_index[:1]
        live = slot < incoming_ref[block // PEER_BLOCKS]
        halo_score_ref[block] = skew(jnp.where(live, source, -jnp.inf))
        return carry

    lax.fori_loop(0, halo_count, halo_table, 0, unroll=32)

    def band_values(tiles):
        parts = []
        for tile in tiles:
            doubled = jnp.concatenate([tile, tile], 0).astype(LOW)
            for lead in range(0, BLK, 2 * SUB):
                parts.append(doubled * mask_ref[lead : lead + 2 * SUB, :])
        return jnp.concatenate(parts, 0)

    def one_block(block):
        nodes = at_block(block)
        upstream = cotangent_ref[:, nodes]
        upstream_wide = upstream.astype(WIDE)
        near = [pairs_ref[block * pair_count + k] for k in range(local_count)]
        far = [pairs_ref[block * pair_count + k] for k in range(local_count, pair_count)]
        counts = [local_counts_ref[block, k : k + 1, :] for k in range(local_count)]
        counts += [remote_counts_ref[block, k : k + 1, :] for k in range(remote_count)]
        target_score = spread(stats_ref[block, 1:2, :])
        pre_self = target_score + spread(stats_ref[block, 0:1, :])
        logit_self = leaky(pre_self)
        pre = [target_score + own_score_ref[index] for index in near]
        pre += [target_score + halo_score_ref[index] for index in far]
        logits = [
            jnp.where(step_index < spread(count), leaky(value), -jnp.inf)
            for value, count in zip(pre, counts)
        ]
        top = logits[0]
        for logit in logits[1:]:
            top = jnp.maximum(top, logit)
        top = jnp.maximum(spread(jnp.max(top, axis=0, keepdims=True)), logit_self)
        raised = [jnp.exp(logit - top) for logit in logits]
        raised_self = jnp.exp(logit_self - top)
        denom = raised[0]
        for value in raised[1:]:
            denom = denom + value
        denom = spread(column_sum(denom)) + raised_self
        scale = 1.0 / denom
        share = [value * scale for value in raised]
        share_self = raised_self * scale
        sources = [own_projt_ref[index] for index in near]
        sources += [halo_projt_ref[index] for index in far]
        summed = None
        for lead in range(0, pair_count, WEIGHT_GROUP):
            group = slice(lead, lead + WEIGHT_GROUP)
            part = jnp.dot(
                jnp.concatenate(sources[group], 1),
                band_values(raised[group]),
                preferred_element_type=WIDE,
            )
            summed = part if summed is None else summed + part
        self_wide = own_projt_ref[block].astype(WIDE)
        aggregate = (summed + raised_self[:1] * self_wide) * scale[:1]
        out_ref[block] = (aggregate + consts_ref[2]).astype(LOW)
        inner = spread(column_sum(upstream_wide * aggregate))
        grad_self = share_self * (spread(stats_ref[block, 2:3, :]) - inner) * slope_of(pre_self)
        total = None
        for pair in range(pair_count):
            if pair < local_count:
                grad_share = band_ref[block, pair]
            else:
                rows = halo_proj_ref[far[pair - local_count]]
                grad_share = band_of(jnp.dot(rows, upstream, preferred_element_type=WIDE))
            grad_pre = share[pair] * (grad_share - inner) * slope_of(pre[pair])
            if pair < local_count:
                own_src_ref[near[pair]] += grad_pre
            else:
                halo_src_ref[far[pair - local_count]] += grad_pre
            total = grad_pre if total is None else total + grad_pre
        own_rows_ref[block, 0:1, :] = grad_self[:1]
        own_rows_ref[block, 1:2, :] = column_sum(total) + grad_self[:1]
        for lead in range(0, pair_count, SHARE_GROUP):
            grad_sources = lax.dot_general(
                upstream,
                band_values(share[lead : lead + SHARE_GROUP]),
                (((1,), (1,)), ((), ())),
                preferred_element_type=WIDE,
            )
            for pair in range(lead, min(lead + SHARE_GROUP, pair_count)):
                grad = grad_sources[:, (pair - lead) * BLK : (pair - lead + 1) * BLK]
                if pair < local_count:
                    own_grad_ref[near[pair]] += grad
                else:
                    halo_grad_ref[far[pair - local_count]] += grad
        own_grad_ref[block] += share_self[:1] * upstream_wide

    def one_turn(turn, carry):
        for part in range(TURN_BLOCKS):
            one_block(turn * TURN_BLOCKS + part)
        return carry

    for fetch in fetches[1:-1]:
        fetch.wait()
    lax.fori_loop(0, block_count // TURN_BLOCKS, one_turn, 0)
    store = pltpu.make_async_copy(out_ref, out_hbm, copy_sem.at[len(fetches)])
    store.start()
    fetches[-1].wait()

    def finish(index, rows, own, carry):
        grad_weight, from_src, from_dst = carry
        parts = []
        for part in range(8):
            at = index * 8 + part
            if own:
                turned = own_projt_ref[at].astype(WIDE)
                source = unskew(own_src_ref[at]) + own_rows_ref[at, 0:1, :]
                target = own_rows_ref[at, 1:2, :]
                grad = own_grad_ref[at] + consts_ref[0] * source + consts_ref[1] * target
                from_dst = from_dst + turned * target
            else:
                turned = halo_projt_ref[at].astype(WIDE)
                source = unskew(halo_src_ref[at])
                grad = halo_grad_ref[at] + consts_ref[0] * source
            from_src = from_src + turned * source
            high = grad.astype(LOW)
            low = (grad - high.astype(WIDE)).astype(LOW)
            parts.append(jnp.concatenate([high, low], 0))
        grad_weight = grad_weight + jnp.dot(
            jnp.concatenate(parts, 1), rows, preferred_element_type=WIDE
        )
        return grad_weight, from_src, from_dst

    def finish_own(index, carry):
        return finish(index, own_ref[at_block(index, 8), :], True, carry)

    def finish_halo(index, carry):
        return finish(index, halo_ref[at_block(index, 8), :], False, carry)

    zero = jnp.zeros((head_width, BLK), WIDE)
    carry = (jnp.zeros((2 * head_width, own_ref.shape[1]), WIDE), zero, zero)
    carry = lax.fori_loop(0, block_count // 8, finish_own, carry, unroll=8)
    carry = lax.fori_loop(0, halo_count // 8, finish_halo, carry, unroll=8)
    grad_weight, from_src, from_dst = carry
    grad_weight = grad_weight[:head_width] + grad_weight[head_width:]
    lanes = lax.broadcasted_iota(jnp.int32, (head_width, BLK), 1)
    extra = jnp.zeros((head_width, BLK), WIDE)
    for place, value in enumerate((from_src, from_dst, bias_ref[...])):
        extra = jnp.where(lanes == place, jnp.sum(value, axis=1, keepdims=True), extra)
    extra = jnp.concatenate([extra, jnp.zeros((BLK - head_width, BLK), WIDE)], 0).T
    for copy in range(shares_ref.shape[0]):
        shares_ref[copy, :head_width, :] = grad_weight
        shares_ref[copy, head_width:, :] = extra[:SUB]
    store.wait()


def relay_kernel(parts_ref, out_ref):
    total = parts_ref[0]
    for part in range(1, parts_ref.shape[0]):
        total = total + parts_ref[part]
    for copy in range(out_ref.shape[0]):
        out_ref[copy] = total


def keep_kernel(sums_ref, out_ref):
    out_ref[...] = sums_ref[0]


def last_kernel(place_ref, parts_ref, kept_ref, weight_ref, attention_ref, bias_ref):
    kept = kept_ref[...]
    total = None
    for part in range(parts_ref.shape[0]):
        value = jnp.where(place_ref[0] == part, kept, parts_ref[part])
        total = value if total is None else total + value
    head_width = weight_ref.shape[0]
    weight_ref[...] = total[:head_width]
    attention_ref[0] = total[head_width : head_width + 1, :head_width]
    attention_ref[1] = total[head_width + 1 : head_width + 2, :head_width]
    bias_ref[...] = total[head_width + 2 : head_width + 3, :head_width]


def vmem():
    return pl.BlockSpec(memory_space=pltpu.VMEM)


def anywhere():
    return pl.BlockSpec(memory_space=pl.ANY)


def smem():
    return pl.BlockSpec(memory_space=pltpu.SMEM)


def gather_rows(rows, live, features):
    slots = rows.shape[0]
    node_count, in_width = features.shape
    return pl.pallas_call(
        gather_kernel,
        out_shape=jax.ShapeDtypeStruct((slots, in_width), LOW),
        in_specs=[smem(), smem(), vmem()],
        out_specs=vmem(),
        scratch_shapes=[
            pltpu.VMEM((node_count, in_width), WIDE),
            pltpu.VMEM((slots, in_width), WIDE),
        ],
        compiler_params=pltpu.CompilerParams(vmem_limit_bytes=VMEM_LIMIT),
        name="gather_rows",
    )(rows, live, features)


def own_part(local_count, *operands):
    pairs, features, weight = operands[:3]
    head_width = weight.shape[1]
    block_count = features.shape[0] // BLK
    tiles = jax.ShapeDtypeStruct((block_count, SUB, BLK), WIDE)
    return pl.pallas_call(
        own_kernel,
        out_shape=(
            jax.ShapeDtypeStruct((block_count, head_width, BLK), LOW),
            tiles,
            tiles,
            jax.ShapeDtypeStruct((block_count, local_count, SUB, BLK), WIDE),
            jax.ShapeDtypeStruct((head_width, BLK), WIDE),
        ),
        in_specs=[smem()] + [vmem()] * 4,
        out_specs=(vmem(),) * 5,
        scratch_shapes=[pltpu.VMEM((block_count, BLK, head_width), LOW)],
        compiler_params=pltpu.CompilerParams(vmem_limit_bytes=OWN_LIMIT),
        cost_estimate=pl.CostEstimate(flops=10**10, bytes_accessed=8 * 10**6, transcendentals=0),
        name="own_part",
    )(*operands)


def attention_layer(*operands):
    incoming, pairs, weight = operands[:3]
    streamed = operands[5:]
    halo, cotangent = streamed[0], streamed[4]
    in_width = halo.shape[1]
    head_width, node_count = cotangent.shape
    block_count = node_count // BLK
    halo_count = halo.shape[0] // BLK
    return pl.pallas_call(
        layer_kernel,
        out_shape=(
            jax.ShapeDtypeStruct((block_count, head_width, BLK), LOW),
            jax.ShapeDtypeStruct((NEAR_GROUP, head_width + SUB, in_width), WIDE),
        ),
        in_specs=[smem()] * 2 + [vmem()] * 3 + [anywhere()] * len(streamed),
        out_specs=(anywhere(), vmem()),
        scratch_shapes=[
            pltpu.VMEM((halo_count, BLK, head_width), LOW),
            pltpu.VMEM((halo_count, head_width, BLK), LOW),
            pltpu.VMEM((halo_count, SUB, BLK), WIDE),
            pltpu.VMEM((block_count, head_width, BLK), WIDE),
            pltpu.VMEM((halo_count, head_width, BLK), WIDE),
            pltpu.VMEM((block_count, SUB, BLK), WIDE),
            pltpu.VMEM((halo_count, SUB, BLK), WIDE),
            pltpu.VMEM((block_count, SUB, BLK), WIDE),
            pltpu.VMEM((BLK, BLK), LOW),
        ]
        + [pltpu.VMEM(value.shape, value.dtype) for value in streamed]
        + [
            pltpu.VMEM((block_count, head_width, BLK), LOW),
            pltpu.SemaphoreType.DMA((len(streamed) + 1,)),
        ],
        compiler_params=pltpu.CompilerParams(vmem_limit_bytes=LAYER_LIMIT),
        cost_estimate=pl.CostEstimate(flops=10**10, bytes_accessed=10**7, transcendentals=0),
        name="attention_layer",
    )(*operands)


def per_device(
    features,
    weight,
    attention,
    bias,
    cotangent,
    local_pairs,
    local_counts,
    remote_pairs,
    remote_counts,
    send_rows,
    send_counts,
):
    node_count, in_width = features.shape
    head_width = weight.shape[1]
    peer_count = lax.axis_size("dom")
    capacity = PEER_BLOCKS * BLK
    slots = peer_count * capacity
    me = lax.axis_index("dom")
    outgoing_live = lax.dynamic_index_in_dim(send_counts, me, 0, False)
    incoming_live = lax.dynamic_index_in_dim(send_counts, me, 1, False)
    outgoing = gather_rows(send_rows.reshape(-1), outgoing_live, features)
    halo = lax.all_to_all(
        outgoing.reshape(peer_count, capacity, in_width), "dom", 0, 0, tiled=True
    ).reshape(slots, in_width)
    consts = jnp.broadcast_to(
        jnp.concatenate([attention[:, 0], bias[None]], 0)[:, :, None], (3, head_width, BLK)
    )
    pairs = jnp.concatenate([local_pairs, remote_pairs], 1).reshape(-1)
    projt, score, stats, band, grad_bias = own_part(
        local_pairs.shape[1], pairs, features, weight, consts, cotangent
    )
    output_blocks, shares = attention_layer(
        incoming_live,
        pairs,
        weight,
        consts,
        grad_bias,
        halo,
        projt,
        score,
        stats,
        cotangent,
        local_counts,
        remote_counts,
        band,
        features,
    )
    near = [list(range(base, base + NEAR_GROUP)) for base in range(0, peer_count, NEAR_GROUP)]
    far = [list(range(base, peer_count, NEAR_GROUP)) for base in range(NEAR_GROUP)]
    output = output_blocks.transpose(1, 0, 2).reshape(head_width, node_count)
    partial_sums, output = lax.optimization_barrier((exchange(shares, near), output))
    group_sums = pl.pallas_call(
        relay_kernel,
        out_shape=jax.ShapeDtypeStruct((peer_count // NEAR_GROUP,) + shares.shape[1:], WIDE),
        in_specs=[vmem()],
        out_specs=vmem(),
        compiler_params=pltpu.CompilerParams(vmem_limit_bytes=SMALL_LIMIT),
        name="relay_sums",
    )(partial_sums)
    kept = pl.pallas_call(
        keep_kernel,
        out_shape=jax.ShapeDtypeStruct(shares.shape[1:], WIDE),
        in_specs=[vmem()],
        out_specs=vmem(),
        compiler_params=pltpu.CompilerParams(vmem_limit_bytes=SMALL_LIMIT),
        name="keep_own",
    )(group_sums)
    grad_weight, grad_attention, grad_bias = pl.pallas_call(
        last_kernel,
        out_shape=(
            jax.ShapeDtypeStruct((head_width, in_width), WIDE),
            jax.ShapeDtypeStruct((2, 1, head_width), WIDE),
            jax.ShapeDtypeStruct((1, head_width), WIDE),
        ),
        in_specs=[smem(), vmem(), vmem()],
        out_specs=(vmem(), vmem(), vmem()),
        compiler_params=pltpu.CompilerParams(vmem_limit_bytes=SMALL_LIMIT),
        name="last_sums",
    )(me[None] // NEAR_GROUP, exchange(group_sums, far), kept)
    return output, grad_weight.T, grad_attention, grad_bias[0]


def exchange(values, groups):
    return lax.all_to_all(values, "dom", 0, 0, tiled=True, axis_index_groups=groups)


def solution(mesh):
    return jax.shard_map(
        per_device,
        mesh=mesh,
        in_specs=(
            P("dom", None),
            P(None, "feat"),
            P(None, "feat", None),
            P("feat"),
            P("feat", "dom"),
            P("dom", None),
            P("dom", None, None),
            P("dom", None),
            P("dom", None, None),
            P("dom", None, None),
            P(),
        ),
        out_specs=(P("feat", "dom"), P(None, "feat"), P(None, "feat", None), P("feat")),
        check_vma=False,
    )
```

```python
import jax
import jax.numpy as jnp
from jax import lax
from jax.experimental import pallas as pl
from jax.experimental.pallas import tpu as pltpu
from jax.sharding import PartitionSpec as P

BLK = 128
PEER_BLOCKS = 2
SUB = 8
LOW = jnp.bfloat16
WIDE = jnp.float32
VMEM_LIMIT = 32 * 1024 * 1024
OWN_LIMIT = 62 * 1024 * 1024
SMALL_LIMIT = 4 * 1024 * 1024
LAYER_LIMIT = 60 * 1024 * 1024
TURN_BLOCKS = 16
NEAR_GROUP = 4
FAR_GROUP = 8
GATHER_PARTS = 4
WEIGHT_GROUP = 8
SHARE_GROUP = 2
GATHER_STEP = 32


def gather_kernel(
    rows_ref, live_ref, features_hbm, out_hbm, features_ref, wide_ref, stage_ref, in_sem, out_sem
):
    node_count = features_ref.shape[0]
    peer_count = live_ref.shape[0]
    capacity = rows_ref.shape[0] // peer_count
    step_count = capacity // GATHER_STEP

    def widen(turn, carry):
        lead = pl.multiple_of(turn * BLK, BLK)
        wide_ref[pl.ds(lead, BLK), :] = features_ref[pl.ds(lead, BLK), :].astype(WIDE)
        return carry

    part_nodes = node_count // GATHER_PARTS
    fetches = []
    for part in range(GATHER_PARTS):
        nodes = pl.ds(part * part_nodes, part_nodes)
        fetches.append(
            pltpu.make_async_copy(features_hbm.at[nodes], features_ref.at[nodes], in_sem.at[part])
        )
        fetches[part].start()
    blocks = part_nodes // BLK
    for part in range(GATHER_PARTS):
        fetches[part].wait()
        lax.fori_loop(part * blocks, (part + 1) * blocks, widen, 0, unroll=4)

    def one_peer(peer, carry):
        busy = (live_ref[peer] + GATHER_STEP - 1) // GATHER_STEP

        def fetch(step, inner):
            lead = pl.multiple_of(peer * capacity + step * GATHER_STEP, GATHER_STEP)
            for slot in range(GATHER_STEP):
                row = rows_ref[lead + slot]
                stage_ref[pl.ds(lead + slot, 1), :] = wide_ref[pl.ds(row, 1), :]
            return inner

        def blank(step, inner):
            lead = pl.multiple_of(peer * capacity + step * GATHER_STEP, GATHER_STEP)
            stage_ref[pl.ds(lead, GATHER_STEP), :] = jnp.zeros((GATHER_STEP, stage_ref.shape[1]), WIDE)
            return inner

        lax.fori_loop(0, busy, fetch, 0)
        lax.fori_loop(busy, step_count, blank, 0)
        return carry

    def narrow(turn, carry):
        lead = pl.multiple_of(turn * BLK, BLK)
        features_ref[pl.ds(lead, BLK), :] = stage_ref[pl.ds(lead, BLK), :].astype(LOW)
        return carry

    part_peers = peer_count // GATHER_PARTS
    part_slots = part_peers * capacity
    stores = []
    for part in range(GATHER_PARTS):
        lax.fori_loop(part * part_peers, (part + 1) * part_peers, one_peer, 0)
        blocks = part_slots // BLK
        lax.fori_loop(part * blocks, (part + 1) * blocks, narrow, 0, unroll=4)
        slots = pl.ds(part * part_slots, part_slots)
        stores.append(
            pltpu.make_async_copy(features_ref.at[slots], out_hbm.at[slots], out_sem.at[part])
        )
        stores[part].start()
    for store in stores:
        store.wait()


def spread(row):
    return jnp.broadcast_to(row, (SUB, BLK))


def leaky(values):
    return jnp.maximum(values, 0.2 * values)


def slope_of(values):
    return jnp.where(values > 0, 1.0, 0.2)


def at_block(index, blocks=1):
    return pl.ds(pl.multiple_of(index * blocks * BLK, BLK), blocks * BLK)


def column_sum(values):
    return jnp.sum(values, axis=0, keepdims=True)


def tile_steps():
    sub_index = lax.broadcasted_iota(jnp.int32, (SUB, BLK), 0)
    lane_index = lax.broadcasted_iota(jnp.int32, (SUB, BLK), 1)
    return (sub_index - lane_index) & (SUB - 1), lane_index


def tile_home():
    sub_index = lax.broadcasted_iota(jnp.int32, (SUB, BLK), 0)
    lane_index = lax.broadcasted_iota(jnp.int32, (SUB, BLK), 1)
    return (lane_index & (SUB - 1)) == sub_index


def skew(row):
    placed = jnp.where(tile_home(), spread(row), 0.0)
    placed = placed + pltpu.roll(placed, BLK - 1, 1)
    placed = placed + pltpu.roll(placed, BLK - 2, 1)
    return placed + pltpu.roll(placed, BLK - 4, 1)


def unskew(tile):
    tile = tile + pltpu.roll(tile, 1, 1)
    tile = tile + pltpu.roll(tile, 2, 1)
    tile = tile + pltpu.roll(tile, 4, 1)
    return column_sum(jnp.where(tile_home(), tile, 0.0))


def band_of(product):
    step_index, lane_index = tile_steps()
    tile_index = ((lane_index + step_index) & (BLK - 1)) // SUB
    band = product[:SUB]
    for part in range(1, BLK // SUB):
        band = jnp.where(tile_index == part, product[part * SUB : (part + 1) * SUB], band)
    return band


def project_into(rows, weight, weight_turned, proj_ref, projt_ref, index):
    proj_ref[index] = jnp.dot(rows, weight, preferred_element_type=WIDE).astype(LOW)
    turned = lax.dot_general(
        weight_turned, rows, (((1,), (1,)), ((), ())), preferred_element_type=WIDE
    ).astype(LOW)
    projt_ref[index] = turned
    return turned.astype(WIDE)


def own_kernel(
    pairs_ref,
    own_ref,
    weight_ref,
    consts_ref,
    cotangent_ref,
    projt_ref,
    score_ref,
    stats_ref,
    band_ref,
    bias_ref,
    proj_ref,
):
    block_count = own_ref.shape[0] // BLK
    local_count = band_ref.shape[1]
    pair_count = pairs_ref.shape[0] // block_count
    weight = weight_ref[...]
    weight_turned = weight.astype(WIDE).T.astype(LOW)

    def one_table(block, grad_bias):
        nodes = at_block(block)
        turned = project_into(own_ref[nodes, :], weight, weight_turned, proj_ref, projt_ref, block)
        source = column_sum(turned * consts_ref[0])
        score_ref[block] = skew(source)
        upstream = cotangent_ref[:, nodes].astype(WIDE)
        stats_ref[block, 0:1, :] = source
        stats_ref[block, 1:2, :] = column_sum(turned * consts_ref[1])
        stats_ref[block, 2:3, :] = column_sum(upstream * turned)
        return grad_bias + upstream

    zero = jnp.zeros((weight.shape[1], BLK), WIDE)
    bias_ref[...] = lax.fori_loop(0, block_count, one_table, zero, unroll=8)

    def one_block(block, carry):
        upstream = cotangent_ref[:, at_block(block)]
        for pair in range(local_count):
            rows = proj_ref[pairs_ref[block * pair_count + pair]]
            band_ref[block, pair] = band_of(jnp.dot(rows, upstream, preferred_element_type=WIDE))
        return carry

    lax.fori_loop(0, block_count, one_block, 0, unroll=2)


def layer_kernel(
    incoming_ref,
    pairs_ref,
    weight_ref,
    consts_ref,
    bias_ref,
    halo_hbm,
    own_projt_hbm,
    own_score_hbm,
    stats_hbm,
    cotangent_hbm,
    local_counts_hbm,
    remote_counts_hbm,
    band_hbm,
    own_hbm,
    out_hbm,
    shares_ref,
    halo_proj_ref,
    halo_projt_ref,
    halo_score_ref,
    own_grad_ref,
    halo_grad_ref,
    own_src_ref,
    halo_src_ref,
    own_rows_ref,
    mask_ref,
    halo_ref,
    own_projt_ref,
    own_score_ref,
    stats_ref,
    cotangent_ref,
    local_counts_ref,
    remote_counts_ref,
    band_ref,
    own_ref,
    out_ref,
    copy_sem,
):
    fetches = []
    for place, (source, target) in enumerate(
        (
            (halo_hbm, halo_ref),
            (own_projt_hbm, own_projt_ref),
            (own_score_hbm, own_score_ref),
            (stats_hbm, stats_ref),
            (cotangent_hbm, cotangent_ref),
            (local_counts_hbm, local_counts_ref),
            (remote_counts_hbm, remote_counts_ref),
            (band_hbm, band_ref),
            (own_hbm, own_ref),
        )
    ):
        fetches.append(pltpu.make_async_copy(source, target, copy_sem.at[place]))
    for fetch in fetches:
        fetch.start()
    block_count = own_ref.shape[0] // BLK
    halo_count = halo_ref.shape[0] // BLK
    local_count = band_ref.shape[1]
    pair_count = pairs_ref.shape[0] // block_count
    remote_count = pair_count - local_count
    head_width = weight_ref.shape[1]
    step_index, lane_index = tile_steps()
    row_all = lax.broadcasted_iota(jnp.int32, (BLK, BLK), 0)
    lane_all = lax.broadcasted_iota(jnp.int32, (BLK, BLK), 1)
    mask_ref[...] = jnp.where(((row_all - lane_all) & (BLK - 1)) < SUB, 1.0, 0.0).astype(LOW)
    weight = weight_ref[...]
    weight_turned = weight.astype(WIDE).T.astype(LOW)

    own_grad_ref[...] = jnp.zeros(own_grad_ref.shape, WIDE)
    halo_grad_ref[...] = jnp.zeros(halo_grad_ref.shape, WIDE)
    own_src_ref[...] = jnp.zeros(own_src_ref.shape, WIDE)
    halo_src_ref[...] = jnp.zeros(halo_src_ref.shape, WIDE)

    fetches[0].wait()

    def halo_table(block, carry):
        rows = halo_ref[at_block(block), :]
        turned = project_into(
            rows, weight, weight_turned, halo_proj_ref, halo_projt_ref, block
        )
        source = column_sum(turned * consts_ref[0])
        slot = (block % PEER_BLOCKS) * BLK + lane_index[:1]
        live = slot < incoming_ref[block // PEER_BLOCKS]
        halo_score_ref[block] = skew(jnp.where(live, source, -jnp.inf))
        return carry

    lax.fori_loop(0, halo_count, halo_table, 0, unroll=32)

    def band_values(tiles):
        parts = []
        for tile in tiles:
            doubled = jnp.concatenate([tile, tile], 0).astype(LOW)
            for lead in range(0, BLK, 2 * SUB):
                parts.append(doubled * mask_ref[lead : lead + 2 * SUB, :])
        return jnp.concatenate(parts, 0)

    def one_block(block):
        nodes = at_block(block)
        upstream = cotangent_ref[:, nodes]
        upstream_wide = upstream.astype(WIDE)
        near = [pairs_ref[block * pair_count + k] for k in range(local_count)]
        far = [pairs_ref[block * pair_count + k] for k in range(local_count, pair_count)]
        counts = [local_counts_ref[block, k : k + 1, :] for k in range(local_count)]
        counts += [remote_counts_ref[block, k : k + 1, :] for k in range(remote_count)]
        target_score = spread(stats_ref[block, 1:2, :])
        pre_self = target_score + spread(stats_ref[block, 0:1, :])
        logit_self = leaky(pre_self)
        pre = [target_score + own_score_ref[index] for index in near]
        pre += [target_score + halo_score_ref[index] for index in far]
        logits = [
            jnp.where(step_index < spread(count), leaky(value), -jnp.inf)
            for value, count in zip(pre, counts)
        ]
        top = logits[0]
        for logit in logits[1:]:
            top = jnp.maximum(top, logit)
        top = jnp.maximum(spread(jnp.max(top, axis=0, keepdims=True)), logit_self)
        raised = [jnp.exp(logit - top) for logit in logits]
        raised_self = jnp.exp(logit_self - top)
        denom = raised[0]
        for value in raised[1:]:
            denom = denom + value
        denom = spread(column_sum(denom)) + raised_self
        scale = 1.0 / denom
        share = [value * scale for value in raised]
        share_self = raised_self * scale
        sources = [own_projt_ref[index] for index in near]
        sources += [halo_projt_ref[index] for index in far]
        summed = None
        for lead in range(0, pair_count, WEIGHT_GROUP):
            group = slice(lead, lead + WEIGHT_GROUP)
            part = jnp.dot(
                jnp.concatenate(sources[group], 1),
                band_values(raised[group]),
                preferred_element_type=WIDE,
            )
            summed = part if summed is None else summed + part
        self_wide = own_projt_ref[block].astype(WIDE)
        aggregate = (summed + raised_self[:1] * self_wide) * scale[:1]
        out_ref[block] = (aggregate + consts_ref[2]).astype(LOW)
        inner = spread(column_sum(upstream_wide * aggregate))
        grad_self = share_self * (spread(stats_ref[block, 2:3, :]) - inner) * slope_of(pre_self)
        total = None
        for pair in range(pair_count):
            if pair < local_count:
                grad_share = band_ref[block, pair]
            else:
                rows = halo_proj_ref[far[pair - local_count]]
                grad_share = band_of(jnp.dot(rows, upstream, preferred_element_type=WIDE))
            grad_pre = share[pair] * (grad_share - inner) * slope_of(pre[pair])
            if pair < local_count:
                own_src_ref[near[pair]] += grad_pre
            else:
                halo_src_ref[far[pair - local_count]] += grad_pre
            total = grad_pre if total is None else total + grad_pre
        own_rows_ref[block, 0:1, :] = grad_self[:1]
        own_rows_ref[block, 1:2, :] = column_sum(total) + grad_self[:1]
        for lead in range(0, pair_count, SHARE_GROUP):
            grad_sources = lax.dot_general(
                upstream,
                band_values(share[lead : lead + SHARE_GROUP]),
                (((1,), (1,)), ((), ())),
                preferred_element_type=WIDE,
            )
            for pair in range(lead, min(lead + SHARE_GROUP, pair_count)):
                grad = grad_sources[:, (pair - lead) * BLK : (pair - lead + 1) * BLK]
                if pair < local_count:
                    own_grad_ref[near[pair]] += grad
                else:
                    halo_grad_ref[far[pair - local_count]] += grad
        own_grad_ref[block] += share_self[:1] * upstream_wide

    def one_turn(turn, carry):
        for part in range(TURN_BLOCKS):
            one_block(turn * TURN_BLOCKS + part)
        return carry

    for fetch in fetches[1:-1]:
        fetch.wait()
    lax.fori_loop(0, block_count // TURN_BLOCKS, one_turn, 0)
    store = pltpu.make_async_copy(out_ref, out_hbm, copy_sem.at[len(fetches)])
    store.start()
    fetches[-1].wait()

    def finish(index, rows, own, carry):
        grad_weight, from_src, from_dst = carry
        parts = []
        for part in range(8):
            at = index * 8 + part
            if own:
                turned = own_projt_ref[at].astype(WIDE)
                source = unskew(own_src_ref[at]) + own_rows_ref[at, 0:1, :]
                target = own_rows_ref[at, 1:2, :]
                grad = own_grad_ref[at] + consts_ref[0] * source + consts_ref[1] * target
                from_dst = from_dst + turned * target
            else:
                turned = halo_projt_ref[at].astype(WIDE)
                source = unskew(halo_src_ref[at])
                grad = halo_grad_ref[at] + consts_ref[0] * source
            from_src = from_src + turned * source
            high = grad.astype(LOW)
            low = (grad - high.astype(WIDE)).astype(LOW)
            parts.append(jnp.concatenate([high, low], 0))
        grad_weight = grad_weight + jnp.dot(
            jnp.concatenate(parts, 1), rows, preferred_element_type=WIDE
        )
        return grad_weight, from_src, from_dst

    def finish_own(index, carry):
        return finish(index, own_ref[at_block(index, 8), :], True, carry)

    def finish_halo(index, carry):
        return finish(index, halo_ref[at_block(index, 8), :], False, carry)

    zero = jnp.zeros((head_width, BLK), WIDE)
    carry = (jnp.zeros((2 * head_width, own_ref.shape[1]), WIDE), zero, zero)
    carry = lax.fori_loop(0, block_count // 8, finish_own, carry, unroll=8)
    carry = lax.fori_loop(0, halo_count // 8, finish_halo, carry, unroll=8)
    grad_weight, from_src, from_dst = carry
    grad_weight = grad_weight[:head_width] + grad_weight[head_width:]
    lanes = lax.broadcasted_iota(jnp.int32, (head_width, BLK), 1)
    extra = jnp.zeros((head_width, BLK), WIDE)
    for place, value in enumerate((from_src, from_dst, bias_ref[...])):
        extra = jnp.where(lanes == place, jnp.sum(value, axis=1, keepdims=True), extra)
    extra = jnp.concatenate([extra, jnp.zeros((BLK - head_width, BLK), WIDE)], 0).T
    for copy in range(shares_ref.shape[0]):
        shares_ref[copy, :head_width, :] = grad_weight
        shares_ref[copy, head_width:, :] = extra[:SUB]
    store.wait()


def relay_kernel(parts_ref, out_ref):
    total = parts_ref[0]
    for part in range(1, parts_ref.shape[0]):
        total = total + parts_ref[part]
    for copy in range(out_ref.shape[0]):
        out_ref[copy] = total


def keep_kernel(sums_ref, out_ref):
    out_ref[...] = sums_ref[0]


def last_kernel(place_ref, parts_ref, kept_ref, weight_ref, attention_ref, bias_ref):
    kept = kept_ref[...]
    total = None
    for part in range(parts_ref.shape[0]):
        value = jnp.where(place_ref[0] == part, kept, parts_ref[part])
        total = value if total is None else total + value
    head_width = weight_ref.shape[0]
    weight_ref[...] = total[:head_width]
    attention_ref[0] = total[head_width : head_width + 1, :head_width]
    attention_ref[1] = total[head_width + 1 : head_width + 2, :head_width]
    bias_ref[...] = total[head_width + 2 : head_width + 3, :head_width]


def vmem():
    return pl.BlockSpec(memory_space=pltpu.VMEM)


def anywhere():
    return pl.BlockSpec(memory_space=pl.ANY)


def smem():
    return pl.BlockSpec(memory_space=pltpu.SMEM)


def gather_rows(rows, live, features):
    slots = rows.shape[0]
    node_count, in_width = features.shape
    return pl.pallas_call(
        gather_kernel,
        out_shape=jax.ShapeDtypeStruct((slots, in_width), LOW),
        in_specs=[smem(), smem(), anywhere()],
        out_specs=anywhere(),
        scratch_shapes=[
            pltpu.VMEM((max(node_count, slots), in_width), LOW),
            pltpu.VMEM((node_count, in_width), WIDE),
            pltpu.VMEM((slots, in_width), WIDE),
            pltpu.SemaphoreType.DMA((GATHER_PARTS,)),
            pltpu.SemaphoreType.DMA((GATHER_PARTS,)),
        ],
        compiler_params=pltpu.CompilerParams(vmem_limit_bytes=LAYER_LIMIT),
        name="gather_rows",
    )(rows, live, features)


def own_part(local_count, *operands):
    pairs, features, weight = operands[:3]
    head_width = weight.shape[1]
    block_count = features.shape[0] // BLK
    tiles = jax.ShapeDtypeStruct((block_count, SUB, BLK), WIDE)
    return pl.pallas_call(
        own_kernel,
        out_shape=(
            jax.ShapeDtypeStruct((block_count, head_width, BLK), LOW),
            tiles,
            tiles,
            jax.ShapeDtypeStruct((block_count, local_count, SUB, BLK), WIDE),
            jax.ShapeDtypeStruct((head_width, BLK), WIDE),
        ),
        in_specs=[smem()] + [vmem()] * 4,
        out_specs=(vmem(),) * 5,
        scratch_shapes=[pltpu.VMEM((block_count, BLK, head_width), LOW)],
        compiler_params=pltpu.CompilerParams(vmem_limit_bytes=OWN_LIMIT),
        cost_estimate=pl.CostEstimate(flops=10**10, bytes_accessed=8 * 10**6, transcendentals=0),
        name="own_part",
    )(*operands)


def attention_layer(*operands):
    incoming, pairs, weight = operands[:3]
    streamed = operands[5:]
    halo, cotangent = streamed[0], streamed[4]
    in_width = halo.shape[1]
    head_width, node_count = cotangent.shape
    block_count = node_count // BLK
    halo_count = halo.shape[0] // BLK
    return pl.pallas_call(
        layer_kernel,
        out_shape=(
            jax.ShapeDtypeStruct((block_count, head_width, BLK), LOW),
            jax.ShapeDtypeStruct((FAR_GROUP, head_width + SUB, in_width), WIDE),
        ),
        in_specs=[smem()] * 2 + [vmem()] * 3 + [anywhere()] * len(streamed),
        out_specs=(anywhere(), vmem()),
        scratch_shapes=[
            pltpu.VMEM((halo_count, BLK, head_width), LOW),
            pltpu.VMEM((halo_count, head_width, BLK), LOW),
            pltpu.VMEM((halo_count, SUB, BLK), WIDE),
            pltpu.VMEM((block_count, head_width, BLK), WIDE),
            pltpu.VMEM((halo_count, head_width, BLK), WIDE),
            pltpu.VMEM((block_count, SUB, BLK), WIDE),
            pltpu.VMEM((halo_count, SUB, BLK), WIDE),
            pltpu.VMEM((block_count, SUB, BLK), WIDE),
            pltpu.VMEM((BLK, BLK), LOW),
        ]
        + [pltpu.VMEM(value.shape, value.dtype) for value in streamed]
        + [
            pltpu.VMEM((block_count, head_width, BLK), LOW),
            pltpu.SemaphoreType.DMA((len(streamed) + 1,)),
        ],
        compiler_params=pltpu.CompilerParams(vmem_limit_bytes=LAYER_LIMIT),
        cost_estimate=pl.CostEstimate(flops=10**10, bytes_accessed=10**7, transcendentals=0),
        name="attention_layer",
    )(*operands)


def per_device(
    features,
    weight,
    attention,
    bias,
    cotangent,
    local_pairs,
    local_counts,
    remote_pairs,
    remote_counts,
    send_rows,
    send_counts,
):
    node_count, in_width = features.shape
    head_width = weight.shape[1]
    peer_count = lax.axis_size("dom")
    capacity = PEER_BLOCKS * BLK
    slots = peer_count * capacity
    me = lax.axis_index("dom")
    outgoing_live = lax.dynamic_index_in_dim(send_counts, me, 0, False)
    incoming_live = lax.dynamic_index_in_dim(send_counts, me, 1, False)
    outgoing = gather_rows(send_rows.reshape(-1), outgoing_live, features)
    halo = lax.all_to_all(
        outgoing.reshape(peer_count, capacity, in_width), "dom", 0, 0, tiled=True
    ).reshape(slots, in_width)
    consts = jnp.broadcast_to(
        jnp.concatenate([attention[:, 0], bias[None]], 0)[:, :, None], (3, head_width, BLK)
    )
    pairs = jnp.concatenate([local_pairs, remote_pairs], 1).reshape(-1)
    projt, score, stats, band, grad_bias = own_part(
        local_pairs.shape[1], pairs, features, weight, consts, cotangent
    )
    output_blocks, shares = attention_layer(
        incoming_live,
        pairs,
        weight,
        consts,
        grad_bias,
        halo,
        projt,
        score,
        stats,
        cotangent,
        local_counts,
        remote_counts,
        band,
        features,
    )
    near = [list(range(base, base + NEAR_GROUP)) for base in range(0, peer_count, NEAR_GROUP)]
    far = [list(range(base, peer_count, NEAR_GROUP)) for base in range(NEAR_GROUP)]
    output = output_blocks.transpose(1, 0, 2).reshape(head_width, node_count)
    partial_sums, output = lax.optimization_barrier((exchange(shares, far), output))
    group_sums = pl.pallas_call(
        relay_kernel,
        out_shape=jax.ShapeDtypeStruct((NEAR_GROUP,) + shares.shape[1:], WIDE),
        in_specs=[vmem()],
        out_specs=vmem(),
        compiler_params=pltpu.CompilerParams(vmem_limit_bytes=SMALL_LIMIT),
        name="relay_sums",
    )(partial_sums)
    kept = pl.pallas_call(
        keep_kernel,
        out_shape=jax.ShapeDtypeStruct(shares.shape[1:], WIDE),
        in_specs=[vmem()],
        out_specs=vmem(),
        compiler_params=pltpu.CompilerParams(vmem_limit_bytes=SMALL_LIMIT),
        name="keep_own",
    )(group_sums)
    grad_weight, grad_attention, grad_bias = pl.pallas_call(
        last_kernel,
        out_shape=(
            jax.ShapeDtypeStruct((head_width, in_width), WIDE),
            jax.ShapeDtypeStruct((2, 1, head_width), WIDE),
            jax.ShapeDtypeStruct((1, head_width), WIDE),
        ),
        in_specs=[smem(), vmem(), vmem()],
        out_specs=(vmem(), vmem(), vmem()),
        compiler_params=pltpu.CompilerParams(vmem_limit_bytes=SMALL_LIMIT),
        name="last_sums",
    )(me[None] % NEAR_GROUP, exchange(group_sums, near), kept)
    return output, grad_weight.T, grad_attention, grad_bias[0]


def exchange(values, groups):
    return lax.all_to_all(values, "dom", 0, 0, tiled=True, axis_index_groups=groups)


def solution(mesh):
    return jax.shard_map(
        per_device,
        mesh=mesh,
        in_specs=(
            P("dom", None),
            P(None, "feat"),
            P(None, "feat", None),
            P("feat"),
            P("feat", "dom"),
            P("dom", None),
            P("dom", None, None),
            P("dom", None),
            P("dom", None, None),
            P("dom", None, None),
            P(),
        ),
        out_specs=(P("feat", "dom"), P(None, "feat"), P(None, "feat", None), P("feat")),
        check_vma=False,
    )
```

```python
import jax
import jax.numpy as jnp
from jax import lax
from jax.experimental import pallas as pl
from jax.experimental.pallas import tpu as pltpu
from jax.sharding import PartitionSpec as P

BLK = 128
PEER_BLOCKS = 2
SUB = 8
LOW = jnp.bfloat16
WIDE = jnp.float32
VMEM_LIMIT = 32 * 1024 * 1024
OWN_LIMIT = 62 * 1024 * 1024
SMALL_LIMIT = 4 * 1024 * 1024
LAYER_LIMIT = 60 * 1024 * 1024
TURN_BLOCKS = 16
NEAR_GROUP = 4
WEIGHT_GROUP = 8
SHARE_GROUP = 2
GATHER_STEP = 32


def gather_kernel(rows_ref, live_ref, features_ref, out_ref, wide_ref, stage_ref):
    node_count = features_ref.shape[0]
    peer_count = live_ref.shape[0]
    capacity = rows_ref.shape[0] // peer_count
    step_count = capacity // GATHER_STEP

    def widen(turn, carry):
        lead = pl.multiple_of(turn * BLK, BLK)
        wide_ref[pl.ds(lead, BLK), :] = features_ref[pl.ds(lead, BLK), :].astype(WIDE)
        return carry

    lax.fori_loop(0, node_count // BLK, widen, 0, unroll=4)

    def one_peer(peer, carry):
        busy = (live_ref[peer] + GATHER_STEP - 1) // GATHER_STEP

        def fetch(step, inner):
            lead = pl.multiple_of(peer * capacity + step * GATHER_STEP, GATHER_STEP)
            for slot in range(GATHER_STEP):
                row = rows_ref[lead + slot]
                stage_ref[pl.ds(lead + slot, 1), :] = wide_ref[pl.ds(row, 1), :]
            return inner

        def blank(step, inner):
            lead = pl.multiple_of(peer * capacity + step * GATHER_STEP, GATHER_STEP)
            stage_ref[pl.ds(lead, GATHER_STEP), :] = jnp.zeros((GATHER_STEP, stage_ref.shape[1]), WIDE)
            return inner

        lax.fori_loop(0, busy, fetch, 0)
        lax.fori_loop(busy, step_count, blank, 0)
        return carry

    lax.fori_loop(0, peer_count, one_peer, 0)

    def narrow(turn, carry):
        lead = pl.multiple_of(turn * BLK, BLK)
        out_ref[pl.ds(lead, BLK), :] = stage_ref[pl.ds(lead, BLK), :].astype(LOW)
        return carry

    lax.fori_loop(0, peer_count * capacity // BLK, narrow, 0, unroll=4)


def spread(row):
    return jnp.broadcast_to(row, (SUB, BLK))


def leaky(values):
    return jnp.maximum(values, 0.2 * values)


def slope_of(values):
    return jnp.where(values > 0, 1.0, 0.2)


def at_block(index, blocks=1):
    return pl.ds(pl.multiple_of(index * blocks * BLK, BLK), blocks * BLK)


def column_sum(values):
    return jnp.sum(values, axis=0, keepdims=True)


def tile_steps():
    sub_index = lax.broadcasted_iota(jnp.int32, (SUB, BLK), 0)
    lane_index = lax.broadcasted_iota(jnp.int32, (SUB, BLK), 1)
    return (sub_index - lane_index) & (SUB - 1), lane_index


def tile_home():
    sub_index = lax.broadcasted_iota(jnp.int32, (SUB, BLK), 0)
    lane_index = lax.broadcasted_iota(jnp.int32, (SUB, BLK), 1)
    return (lane_index & (SUB - 1)) == sub_index


def skew(row):
    placed = jnp.where(tile_home(), spread(row), 0.0)
    placed = placed + pltpu.roll(placed, BLK - 1, 1)
    placed = placed + pltpu.roll(placed, BLK - 2, 1)
    return placed + pltpu.roll(placed, BLK - 4, 1)


def unskew(tile):
    tile = tile + pltpu.roll(tile, 1, 1)
    tile = tile + pltpu.roll(tile, 2, 1)
    tile = tile + pltpu.roll(tile, 4, 1)
    return column_sum(jnp.where(tile_home(), tile, 0.0))


def band_of(product):
    step_index, lane_index = tile_steps()
    tile_index = ((lane_index + step_index) & (BLK - 1)) // SUB
    band = product[:SUB]
    for part in range(1, BLK // SUB):
        band = jnp.where(tile_index == part, product[part * SUB : (part + 1) * SUB], band)
    return band


def project_into(rows, weight, weight_turned, proj_ref, projt_ref, index):
    proj_ref[index] = jnp.dot(rows, weight, preferred_element_type=WIDE).astype(LOW)
    turned = lax.dot_general(
        weight_turned, rows, (((1,), (1,)), ((), ())), preferred_element_type=WIDE
    ).astype(LOW)
    projt_ref[index] = turned
    return turned.astype(WIDE)


def own_kernel(
    pairs_ref,
    own_ref,
    weight_ref,
    consts_ref,
    cotangent_ref,
    projt_ref,
    score_ref,
    stats_ref,
    band_ref,
    bias_ref,
    proj_ref,
):
    block_count = own_ref.shape[0] // BLK
    local_count = band_ref.shape[1]
    pair_count = pairs_ref.shape[0] // block_count
    weight = weight_ref[...]
    weight_turned = weight.astype(WIDE).T.astype(LOW)

    def one_table(block, grad_bias):
        nodes = at_block(block)
        turned = project_into(own_ref[nodes, :], weight, weight_turned, proj_ref, projt_ref, block)
        source = column_sum(turned * consts_ref[0])
        score_ref[block] = skew(source)
        upstream = cotangent_ref[:, nodes].astype(WIDE)
        stats_ref[block, 0:1, :] = source
        stats_ref[block, 1:2, :] = column_sum(turned * consts_ref[1])
        stats_ref[block, 2:3, :] = column_sum(upstream * turned)
        return grad_bias + upstream

    zero = jnp.zeros((weight.shape[1], BLK), WIDE)
    bias_ref[...] = lax.fori_loop(0, block_count, one_table, zero, unroll=8)

    def one_block(block, carry):
        upstream = cotangent_ref[:, at_block(block)]
        for pair in range(local_count):
            rows = proj_ref[pairs_ref[block * pair_count + pair]]
            band_ref[block, pair] = band_of(jnp.dot(rows, upstream, preferred_element_type=WIDE))
        return carry

    lax.fori_loop(0, block_count, one_block, 0, unroll=2)


def layer_kernel(
    incoming_ref,
    pairs_ref,
    weight_ref,
    consts_ref,
    bias_ref,
    halo_hbm,
    own_projt_hbm,
    own_score_hbm,
    stats_hbm,
    cotangent_hbm,
    local_counts_hbm,
    remote_counts_hbm,
    band_hbm,
    own_hbm,
    out_hbm,
    shares_ref,
    halo_proj_ref,
    halo_projt_ref,
    halo_score_ref,
    own_grad_ref,
    halo_grad_ref,
    own_src_ref,
    halo_src_ref,
    own_rows_ref,
    mask_ref,
    halo_ref,
    own_projt_ref,
    own_score_ref,
    stats_ref,
    cotangent_ref,
    local_counts_ref,
    remote_counts_ref,
    band_ref,
    own_ref,
    out_ref,
    copy_sem,
):
    fetches = []
    for place, (source, target) in enumerate(
        (
            (halo_hbm, halo_ref),
            (own_projt_hbm, own_projt_ref),
            (own_score_hbm, own_score_ref),
            (stats_hbm, stats_ref),
            (cotangent_hbm, cotangent_ref),
            (local_counts_hbm, local_counts_ref),
            (remote_counts_hbm, remote_counts_ref),
            (band_hbm, band_ref),
            (own_hbm, own_ref),
        )
    ):
        fetches.append(pltpu.make_async_copy(source, target, copy_sem.at[place]))
    for fetch in fetches:
        fetch.start()
    block_count = own_ref.shape[0] // BLK
    halo_count = halo_ref.shape[0] // BLK
    local_count = band_ref.shape[1]
    pair_count = pairs_ref.shape[0] // block_count
    remote_count = pair_count - local_count
    head_width = weight_ref.shape[1]
    step_index, lane_index = tile_steps()
    row_all = lax.broadcasted_iota(jnp.int32, (BLK, BLK), 0)
    lane_all = lax.broadcasted_iota(jnp.int32, (BLK, BLK), 1)
    mask_ref[...] = jnp.where(((row_all - lane_all) & (BLK - 1)) < SUB, 1.0, 0.0).astype(LOW)
    weight = weight_ref[...]
    weight_turned = weight.astype(WIDE).T.astype(LOW)

    own_grad_ref[...] = jnp.zeros(own_grad_ref.shape, WIDE)
    halo_grad_ref[...] = jnp.zeros(halo_grad_ref.shape, WIDE)
    own_src_ref[...] = jnp.zeros(own_src_ref.shape, WIDE)
    halo_src_ref[...] = jnp.zeros(halo_src_ref.shape, WIDE)

    fetches[0].wait()

    def halo_table(block, carry):
        rows = halo_ref[at_block(block), :]
        turned = project_into(
            rows, weight, weight_turned, halo_proj_ref, halo_projt_ref, block
        )
        source = column_sum(turned * consts_ref[0])
        slot = (block % PEER_BLOCKS) * BLK + lane_index[:1]
        live = slot < incoming_ref[block // PEER_BLOCKS]
        halo_score_ref[block] = skew(jnp.where(live, source, -jnp.inf))
        return carry

    lax.fori_loop(0, halo_count, halo_table, 0, unroll=32)

    def band_values(tiles):
        parts = []
        for tile in tiles:
            doubled = jnp.concatenate([tile, tile], 0).astype(LOW)
            for lead in range(0, BLK, 2 * SUB):
                parts.append(doubled * mask_ref[lead : lead + 2 * SUB, :])
        return jnp.concatenate(parts, 0)

    def one_block(block):
        nodes = at_block(block)
        upstream = cotangent_ref[:, nodes]
        upstream_wide = upstream.astype(WIDE)
        near = [pairs_ref[block * pair_count + k] for k in range(local_count)]
        far = [pairs_ref[block * pair_count + k] for k in range(local_count, pair_count)]
        counts = [local_counts_ref[block, k : k + 1, :] for k in range(local_count)]
        counts += [remote_counts_ref[block, k : k + 1, :] for k in range(remote_count)]
        target_score = spread(stats_ref[block, 1:2, :])
        pre_self = target_score + spread(stats_ref[block, 0:1, :])
        logit_self = leaky(pre_self)
        pre = [target_score + own_score_ref[index] for index in near]
        pre += [target_score + halo_score_ref[index] for index in far]
        logits = [
            jnp.where(step_index < spread(count), leaky(value), -jnp.inf)
            for value, count in zip(pre, counts)
        ]
        top = logits[0]
        for logit in logits[1:]:
            top = jnp.maximum(top, logit)
        top = jnp.maximum(spread(jnp.max(top, axis=0, keepdims=True)), logit_self)
        raised = [jnp.exp(logit - top) for logit in logits]
        raised_self = jnp.exp(logit_self - top)
        denom = raised[0]
        for value in raised[1:]:
            denom = denom + value
        denom = spread(column_sum(denom)) + raised_self
        scale = 1.0 / denom
        share = [value * scale for value in raised]
        share_self = raised_self * scale
        sources = [own_projt_ref[index] for index in near]
        sources += [halo_projt_ref[index] for index in far]
        summed = None
        for lead in range(0, pair_count, WEIGHT_GROUP):
            group = slice(lead, lead + WEIGHT_GROUP)
            part = jnp.dot(
                jnp.concatenate(sources[group], 1),
                band_values(raised[group]),
                preferred_element_type=WIDE,
            )
            summed = part if summed is None else summed + part
        self_wide = own_projt_ref[block].astype(WIDE)
        aggregate = (summed + raised_self[:1] * self_wide) * scale[:1]
        out_ref[block] = (aggregate + consts_ref[2]).astype(LOW)
        inner = spread(column_sum(upstream_wide * aggregate))
        grad_self = share_self * (spread(stats_ref[block, 2:3, :]) - inner) * slope_of(pre_self)
        total = None
        for pair in range(pair_count):
            if pair < local_count:
                grad_share = band_ref[block, pair]
            else:
                rows = halo_proj_ref[far[pair - local_count]]
                grad_share = band_of(jnp.dot(rows, upstream, preferred_element_type=WIDE))
            grad_pre = share[pair] * (grad_share - inner) * slope_of(pre[pair])
            if pair < local_count:
                own_src_ref[near[pair]] += grad_pre
            else:
                halo_src_ref[far[pair - local_count]] += grad_pre
            total = grad_pre if total is None else total + grad_pre
        own_rows_ref[block, 0:1, :] = grad_self[:1]
        own_rows_ref[block, 1:2, :] = column_sum(total) + grad_self[:1]
        for lead in range(0, pair_count, SHARE_GROUP):
            grad_sources = lax.dot_general(
                upstream,
                band_values(share[lead : lead + SHARE_GROUP]),
                (((1,), (1,)), ((), ())),
                preferred_element_type=WIDE,
            )
            for pair in range(lead, min(lead + SHARE_GROUP, pair_count)):
                grad = grad_sources[:, (pair - lead) * BLK : (pair - lead + 1) * BLK]
                if pair < local_count:
                    own_grad_ref[near[pair]] += grad
                else:
                    halo_grad_ref[far[pair - local_count]] += grad
        own_grad_ref[block] += share_self[:1] * upstream_wide

    def one_turn(turn, carry):
        for part in range(TURN_BLOCKS):
            one_block(turn * TURN_BLOCKS + part)
        return carry

    for fetch in fetches[1:-1]:
        fetch.wait()
    lax.fori_loop(0, block_count // TURN_BLOCKS, one_turn, 0)
    store = pltpu.make_async_copy(out_ref, out_hbm, copy_sem.at[len(fetches)])
    store.start()
    fetches[-1].wait()

    def finish(index, rows, own, carry):
        grad_weight, from_src, from_dst = carry
        parts = []
        for part in range(8):
            at = index * 8 + part
            if own:
                turned = own_projt_ref[at].astype(WIDE)
                source = unskew(own_src_ref[at]) + own_rows_ref[at, 0:1, :]
                target = own_rows_ref[at, 1:2, :]
                grad = own_grad_ref[at] + consts_ref[0] * source + consts_ref[1] * target
                from_dst = from_dst + turned * target
            else:
                turned = halo_projt_ref[at].astype(WIDE)
                source = unskew(halo_src_ref[at])
                grad = halo_grad_ref[at] + consts_ref[0] * source
            from_src = from_src + turned * source
            high = grad.astype(LOW)
            low = (grad - high.astype(WIDE)).astype(LOW)
            parts.append(jnp.concatenate([high, low], 0))
        grad_weight = grad_weight + jnp.dot(
            jnp.concatenate(parts, 1), rows, preferred_element_type=WIDE
        )
        return grad_weight, from_src, from_dst

    def finish_own(index, carry):
        return finish(index, own_ref[at_block(index, 8), :], True, carry)

    def finish_halo(index, carry):
        return finish(index, halo_ref[at_block(index, 8), :], False, carry)

    zero = jnp.zeros((head_width, BLK), WIDE)
    carry = (jnp.zeros((2 * head_width, own_ref.shape[1]), WIDE), zero, zero)
    carry = lax.fori_loop(0, block_count // 8, finish_own, carry, unroll=8)
    carry = lax.fori_loop(0, halo_count // 8, finish_halo, carry, unroll=8)
    grad_weight, from_src, from_dst = carry
    grad_weight = grad_weight[:head_width] + grad_weight[head_width:]
    lanes = lax.broadcasted_iota(jnp.int32, (head_width, BLK), 1)
    extra = jnp.zeros((head_width, BLK), WIDE)
    for place, value in enumerate((from_src, from_dst, bias_ref[...])):
        extra = jnp.where(lanes == place, jnp.sum(value, axis=1, keepdims=True), extra)
    extra = jnp.concatenate([extra, jnp.zeros((BLK - head_width, BLK), WIDE)], 0).T
    for copy in range(shares_ref.shape[0]):
        shares_ref[copy, :head_width, :] = grad_weight
        shares_ref[copy, head_width:, :] = extra[:SUB]
    store.wait()


def relay_kernel(place_ref, parts_ref, kept_ref, out_ref):
    kept = kept_ref[...]
    total = None
    for part in range(parts_ref.shape[0]):
        value = jnp.where(place_ref[0] == part, kept, parts_ref[part])
        total = value if total is None else total + value
    for copy in range(out_ref.shape[0]):
        out_ref[copy] = total


def keep_kernel(sums_ref, out_ref):
    out_ref[...] = sums_ref[0]


def last_kernel(parts_ref, weight_ref, attention_ref, bias_ref):
    total = parts_ref[0]
    for part in range(1, parts_ref.shape[0]):
        total = total + parts_ref[part]
    head_width = weight_ref.shape[0]
    weight_ref[...] = total[:head_width]
    attention_ref[0] = total[head_width : head_width + 1, :head_width]
    attention_ref[1] = total[head_width + 1 : head_width + 2, :head_width]
    bias_ref[...] = total[head_width + 2 : head_width + 3, :head_width]


def vmem():
    return pl.BlockSpec(memory_space=pltpu.VMEM)


def anywhere():
    return pl.BlockSpec(memory_space=pl.ANY)


def smem():
    return pl.BlockSpec(memory_space=pltpu.SMEM)


def gather_rows(rows, live, features):
    slots = rows.shape[0]
    node_count, in_width = features.shape
    return pl.pallas_call(
        gather_kernel,
        out_shape=jax.ShapeDtypeStruct((slots, in_width), LOW),
        in_specs=[smem(), smem(), vmem()],
        out_specs=vmem(),
        scratch_shapes=[
            pltpu.VMEM((node_count, in_width), WIDE),
            pltpu.VMEM((slots, in_width), WIDE),
        ],
        compiler_params=pltpu.CompilerParams(vmem_limit_bytes=VMEM_LIMIT),
        name="gather_rows",
    )(rows, live, features)


def own_part(local_count, *operands):
    pairs, features, weight = operands[:3]
    head_width = weight.shape[1]
    block_count = features.shape[0] // BLK
    tiles = jax.ShapeDtypeStruct((block_count, SUB, BLK), WIDE)
    return pl.pallas_call(
        own_kernel,
        out_shape=(
            jax.ShapeDtypeStruct((block_count, head_width, BLK), LOW),
            tiles,
            tiles,
            jax.ShapeDtypeStruct((block_count, local_count, SUB, BLK), WIDE),
            jax.ShapeDtypeStruct((head_width, BLK), WIDE),
        ),
        in_specs=[smem()] + [vmem()] * 4,
        out_specs=(vmem(),) * 5,
        scratch_shapes=[pltpu.VMEM((block_count, BLK, head_width), LOW)],
        compiler_params=pltpu.CompilerParams(vmem_limit_bytes=OWN_LIMIT),
        cost_estimate=pl.CostEstimate(flops=10**10, bytes_accessed=8 * 10**6, transcendentals=0),
        name="own_part",
    )(*operands)


def attention_layer(*operands):
    incoming, pairs, weight = operands[:3]
    streamed = operands[5:]
    halo, cotangent = streamed[0], streamed[4]
    in_width = halo.shape[1]
    head_width, node_count = cotangent.shape
    block_count = node_count // BLK
    halo_count = halo.shape[0] // BLK
    return pl.pallas_call(
        layer_kernel,
        out_shape=(
            jax.ShapeDtypeStruct((block_count, head_width, BLK), LOW),
            jax.ShapeDtypeStruct((NEAR_GROUP, head_width + SUB, in_width), WIDE),
        ),
        in_specs=[smem()] * 2 + [vmem()] * 3 + [anywhere()] * len(streamed),
        out_specs=(anywhere(), vmem()),
        scratch_shapes=[
            pltpu.VMEM((halo_count, BLK, head_width), LOW),
            pltpu.VMEM((halo_count, head_width, BLK), LOW),
            pltpu.VMEM((halo_count, SUB, BLK), WIDE),
            pltpu.VMEM((block_count, head_width, BLK), WIDE),
            pltpu.VMEM((halo_count, head_width, BLK), WIDE),
            pltpu.VMEM((block_count, SUB, BLK), WIDE),
            pltpu.VMEM((halo_count, SUB, BLK), WIDE),
            pltpu.VMEM((block_count, SUB, BLK), WIDE),
            pltpu.VMEM((BLK, BLK), LOW),
        ]
        + [pltpu.VMEM(value.shape, value.dtype) for value in streamed]
        + [
            pltpu.VMEM((block_count, head_width, BLK), LOW),
            pltpu.SemaphoreType.DMA((len(streamed) + 1,)),
        ],
        compiler_params=pltpu.CompilerParams(vmem_limit_bytes=LAYER_LIMIT),
        cost_estimate=pl.CostEstimate(flops=10**10, bytes_accessed=10**7, transcendentals=0),
        name="attention_layer",
    )(*operands)


def per_device(
    features,
    weight,
    attention,
    bias,
    cotangent,
    local_pairs,
    local_counts,
    remote_pairs,
    remote_counts,
    send_rows,
    send_counts,
):
    node_count, in_width = features.shape
    head_width = weight.shape[1]
    peer_count = lax.axis_size("dom")
    capacity = PEER_BLOCKS * BLK
    slots = peer_count * capacity
    me = lax.axis_index("dom")
    outgoing_live = lax.dynamic_index_in_dim(send_counts, me, 0, False)
    incoming_live = lax.dynamic_index_in_dim(send_counts, me, 1, False)
    outgoing = gather_rows(send_rows.reshape(-1), outgoing_live, features)
    halo = lax.all_to_all(
        outgoing.reshape(peer_count, capacity, in_width), "dom", 0, 0, tiled=True
    ).reshape(slots, in_width)
    consts = jnp.broadcast_to(
        jnp.concatenate([attention[:, 0], bias[None]], 0)[:, :, None], (3, head_width, BLK)
    )
    pairs = jnp.concatenate([local_pairs, remote_pairs], 1).reshape(-1)
    projt, score, stats, band, grad_bias = own_part(
        local_pairs.shape[1], pairs, features, weight, consts, cotangent
    )
    output_blocks, shares = attention_layer(
        incoming_live,
        pairs,
        weight,
        consts,
        grad_bias,
        halo,
        projt,
        score,
        stats,
        cotangent,
        local_counts,
        remote_counts,
        band,
        features,
    )
    near = [list(range(base, base + NEAR_GROUP)) for base in range(0, peer_count, NEAR_GROUP)]
    far = [list(range(base, peer_count, NEAR_GROUP)) for base in range(NEAR_GROUP)]
    kept = pl.pallas_call(
        keep_kernel,
        out_shape=jax.ShapeDtypeStruct(shares.shape[1:], WIDE),
        in_specs=[vmem()],
        out_specs=vmem(),
        compiler_params=pltpu.CompilerParams(vmem_limit_bytes=SMALL_LIMIT),
        name="keep_own",
    )(shares)
    group_sums = pl.pallas_call(
        relay_kernel,
        out_shape=jax.ShapeDtypeStruct((peer_count // NEAR_GROUP,) + shares.shape[1:], WIDE),
        in_specs=[smem(), vmem(), vmem()],
        out_specs=vmem(),
        compiler_params=pltpu.CompilerParams(vmem_limit_bytes=SMALL_LIMIT),
        name="relay_sums",
    )(me[None] % NEAR_GROUP, exchange(shares, near), kept)
    group_sums, output_blocks = lax.optimization_barrier((group_sums, output_blocks))
    output = output_blocks.transpose(1, 0, 2).reshape(head_width, node_count)
    grad_weight, grad_attention, grad_bias = pl.pallas_call(
        last_kernel,
        out_shape=(
            jax.ShapeDtypeStruct((head_width, in_width), WIDE),
            jax.ShapeDtypeStruct((2, 1, head_width), WIDE),
            jax.ShapeDtypeStruct((1, head_width), WIDE),
        ),
        in_specs=[vmem()],
        out_specs=(vmem(), vmem(), vmem()),
        compiler_params=pltpu.CompilerParams(vmem_limit_bytes=SMALL_LIMIT),
        name="last_sums",
    )(exchange(group_sums, far))
    return output, grad_weight.T, grad_attention, grad_bias[0]


def exchange(values, groups):
    return lax.all_to_all(values, "dom", 0, 0, tiled=True, axis_index_groups=groups)


def solution(mesh):
    return jax.shard_map(
        per_device,
        mesh=mesh,
        in_specs=(
            P("dom", None),
            P(None, "feat"),
            P(None, "feat", None),
            P("feat"),
            P("feat", "dom"),
            P("dom", None),
            P("dom", None, None),
            P("dom", None),
            P("dom", None, None),
            P("dom", None, None),
            P(),
        ),
        out_specs=(P("feat", "dom"), P(None, "feat"), P(None, "feat", None), P("feat")),
        check_vma=False,
    )
```
